128 devices in a mesh: ctx: 16 (over z, x), tp: 8 (over y, core).
Axes of the slice: x: 4, y: 4, z: 4, core: 2. Of those that a mesh axis runs over, the one named last changes fastest.
Arguments:
- x_resid: bfloat16 [2048, 7168], P('ctx', 'tp'), may hold values from -4.5 to 4.5
- query_nope: bfloat16 [2048, 8192], P('ctx', 'tp'), may hold values from -6 to 6
- query_rope: bfloat16 [2048, 4096], P('ctx', 'tp'), may hold values from -8 to 8
- latent_kv: bfloat16 [512, 2048], P(None, 'ctx'), may hold values from -6 to 6
- key_rope: bfloat16 [64, 2048], P(None, 'ctx'), may hold values from -8 to 8
- absorb_key: bfloat16 [64, 128, 512], P('tp'), may hold values from -0.5 to 0.5
- absorb_value: bfloat16 [64, 512, 128], P('tp'), may hold values from -0.25 to 0.25
- out_proj: bfloat16 [8192, 7168], P('tp'), may hold values from -0.0625 to 0.0625
- norm_gain: bfloat16 [7168], replicated, may hold values from 0.099609375 to 1.8984375
- router: bfloat16 [16, 7168], replicated, may hold values from -0.0625 to 0.0625
- routes: int32 [2048, 4], P('ctx'), may hold values from 0 to 15, all different within a row; in each aligned block of 128 rows (0 to 127, 128 to 255, ...) at most 64 rows name the same one
- gate_proj: bfloat16 [16, 7168, 1024], P('ctx', None, 'tp'), may hold values from -0.0625 to 0.0625
- up_proj: bfloat16 [16, 7168, 1024], P('ctx', None, 'tp'), may hold values from -0.0625 to 0.0625
- down_proj: bfloat16 [16, 1024, 7168], P('ctx', 'tp'), may hold values from -0.1875 to 0.1875
Outputs:
- layer_out: bfloat16 [2048, 7168], P('ctx', 'tp')
The draws below stay inside these ranges and needn't reach their ends.
Inputs may be any that keep to these rules, and one draw needn't show every extreme that they name: `routes`: each row names 4 different experts; within the rows of one index of ctx no expert is named by more than 64 rows, and that many is reached.
All inputs are finite; a program needn't handle non-finite values.
Results may differ from the reference program's by a relative error of at most 0.033.
Values may be sent and summed in bfloat16 or wider, within the bound.
No kernel may reach another device: no remote copies, remote signals or barrier semaphores. Data moves between devices by JAX's collectives and lax.ppermute only.
A program may use at most 192 MiB of HBM per device.

```python
import math
import jax
import jax.numpy as jnp
import numpy as np
from jax import lax

D = 7168
HEADS = 64
NOPE = 128
ROPE = 64
LATENT = 512
VDIM = 128
EXP_HID = 1024
TOP = 4
TOK_DEV = 128
TOKENS = 2048
EXPERTS = 16
CAP = 64
N_CTX = 16
N_TP = 8


def draw_x_resid(key, part):
    key = jax.random.fold_in(key, 5)
    first_key = jax.random.fold_in(key, 0)
    col_frac = (jnp.arange(D, dtype=jnp.float32) + 0.5) / D
    noise = jax.random.truncated_normal(first_key, -6.0, 6.0, (TOKENS, D), jnp.float32)
    return (noise * (0.25 + 0.5 * col_frac)[None, :]).astype(jnp.bfloat16)


def draw_query_rope(key, part):
    key = jax.random.fold_in(key, 7)
    return jax.random.truncated_normal(key, -8.0, 8.0, (TOKENS, HEADS * ROPE), jnp.float32).astype(jnp.bfloat16)


def draw_key_rope(key, part):
    key = jax.random.fold_in(key, 9)
    return jax.random.truncated_normal(key, -8.0, 8.0, (ROPE, TOKENS), jnp.float32).astype(jnp.bfloat16)


def block_scale(rng, shape, pieces, least, top_value):
    def one(dim, blocks):
        draws = jax.random.uniform(jax.random.fold_in(jax.random.fold_in(rng, 6), dim), (blocks,), jnp.float32, least / len(pieces), top_value / len(pieces))
        return jnp.repeat(jnp.exp(draws), shape[dim] // blocks).reshape((-1,) + (1,) * (len(shape) - dim - 1))

    factor_of = one(*pieces[0])
    for cut in pieces[1:]:
        factor_of = factor_of * one(*cut)
    return factor_of


def routed_block(rng, own, number, rows, amount, top, bound, slope):
    ranking = jax.random.permutation(rng, amount)
    packed, usual = shares(amount, rows * top, bound, slope, True), shares(amount, rows * top, bound, slope, False)
    places = jnp.arange(amount)

    def named(tallies, turn):
        used = int((tallies > 0).sum())
        fixed = max(1, used // 4)
        passed = fixed + (places - fixed + turn * (used - fixed)) % max(1, amount - fixed)
        return jnp.zeros((amount,), jnp.int32).at[ranking[jnp.where(places < fixed, places, passed)]].set(jnp.asarray(tallies, jnp.int32))

    tallies = jnp.where(number % 4 == 0, named(packed, number // 4), named(usual, number - number // 4 - 1))
    mixed = jax.random.permutation(jax.random.fold_in(own, 3), amount)
    giver, receiver = mixed[0:amount // 2 * 2:2], mixed[1:amount // 2 * 2:2]
    margin = jnp.minimum(tallies[giver] - 1, bound - tallies[receiver]) // 2
    margin = jnp.where((giver == ranking[0]) | (receiver == ranking[0]) | (tallies[receiver] == 0), 0, jnp.maximum(margin, 0))
    passed = jax.random.randint(jax.random.fold_in(own, 4), (amount // 2,), 0, 1 << 20) % (margin + 1)
    tallies = tallies.at[giver].add(-passed).at[receiver].add(passed)
    members = jnp.searchsorted(jnp.cumsum(tallies), jnp.arange(rows * top), side="right").astype(jnp.int32)
    table = members.reshape(top, rows).T
    table = table[jax.random.permutation(jax.random.fold_in(own, 1), rows)]
    turn = jax.random.randint(jax.random.fold_in(own, 2), (rows, 1), 0, top)
    return jnp.take_along_axis(table, (jnp.arange(top)[None, :] + turn) % top, axis=1)


def shares(number_of, total, limit, slope, full):
    weights = [(1 << 20) // math.isqrt(standing ** slope) + 1 for standing in range(1, number_of + 1)]
    largest = limit if full else min(limit, max(-(-total // number_of), total * weights[0] // sum(weights)))
    least = 1 if total - largest >= number_of - 1 else 0
    counts, rest = [largest] + [least] * (number_of - 1), total - largest - least * (number_of - 1)
    while rest > 0:
        free = [i for i in range(1, number_of) if counts[i] < largest] or [i for i in range(1, number_of) if counts[i] < limit]
        mass, budget = sum([weights[i] for i in free]), rest
        for i in free:
            more = min(limit - counts[i], max(1, budget * weights[i] // mass), rest)
            counts[i] = counts[i] + more
            rest = rest - more
    return np.array(counts)


def gaussian(key, shape, width, most, cuts=(), kind=jnp.bfloat16):
    values = width * jax.random.normal(key, shape, jnp.float32)
    if cuts:
        values = values * block_scale(key, shape, cuts, -0.22, 0.18)
    return jnp.clip(values, -most, most).astype(kind)


def setup_inputs(seed: int = 0) -> dict:
    key_of = jax.random.split(jax.random.key(seed), 15)
    x_resid = draw_x_resid(jax.random.fold_in(key_of[14], 71), 0)
    query_nope = gaussian(key_of[1], (TOKENS, HEADS * NOPE), 1.0, 6.0, ((0, 16), (1, 8)))
    query_rope = draw_query_rope(jax.random.fold_in(key_of[14], 71), 0)
    latent_kv = gaussian(key_of[3], (LATENT, TOKENS), 1.0, 6.0, ((1, 16),))
    key_rope = draw_key_rope(jax.random.fold_in(key_of[14], 71), 0)
    absorb_key = gaussian(key_of[5], (HEADS, NOPE, LATENT), NOPE ** -0.5, 0.5, ((0, 8),))
    absorb_value = gaussian(key_of[6], (HEADS, LATENT, VDIM), LATENT ** -0.5, 0.25, ((0, 8),))
    out_proj = gaussian(key_of[7], (HEADS * VDIM, D), (HEADS * VDIM) ** -0.5, 0.0625, ((0, 8),))
    norm_gain = jnp.clip(1.0 + 0.18 * jax.random.normal(key_of[8], (D,), jnp.float32), 0.099609375, 1.8984375).astype(jnp.bfloat16)
    router = gaussian(key_of[9], (EXPERTS, D), D ** -0.5, 0.0625)
    routes_keys = jax.random.split(jax.random.fold_in(key_of[10], 1), TOKENS // TOK_DEV)
    routes_turns = jax.random.permutation(jax.random.fold_in(key_of[10], 3), TOKENS // TOK_DEV)
    routes = jax.vmap(lambda own, number: routed_block(jax.random.fold_in(key_of[10], 2), own, number, TOK_DEV, EXPERTS, TOP, CAP, 2))(routes_keys, routes_turns).reshape((TOKENS, TOP))
    gate_proj = gaussian(key_of[11], (EXPERTS, D, EXP_HID), D ** -0.5, 0.0625, ((0, 16), (2, 8)))
    up_proj = gaussian(key_of[12], (EXPERTS, D, EXP_HID), D ** -0.5, 0.0625, ((0, 16), (2, 8)))
    down_proj = gaussian(key_of[13], (EXPERTS, EXP_HID, D), EXP_HID ** -0.5, 0.1875, ((0, 16), (1, 8)))
    return dict(x_resid=x_resid, query_nope=query_nope, query_rope=query_rope, latent_kv=latent_kv, key_rope=key_rope, absorb_key=absorb_key, absorb_value=absorb_value, out_proj=out_proj, norm_gain=norm_gain, router=router, routes=routes, gate_proj=gate_proj, up_proj=up_proj, down_proj=down_proj)


EPS = 1e-06
ROUTE_SCALE = 2.5
LOW_SCORE = -1e+30

def reference(x_resid, query_nope, query_rope, latent_kv, key_rope, absorb_key, absorb_value, out_proj, norm_gain, router, routes, gate_proj, up_proj, down_proj):
    row_count = x_resid.shape[0]
    head_count = absorb_key.shape[0]
    query_lat = jnp.einsum('thn,hnl->thl', query_nope.reshape(row_count, head_count, NOPE).astype(jnp.float32), absorb_key.astype(jnp.float32))
    query_lat = lax.optimization_barrier(query_lat.astype(jnp.bfloat16)).astype(jnp.float32)
    query_rot = query_rope.reshape(row_count, head_count, ROPE).astype(jnp.float32)
    score_scale = (NOPE + ROPE) ** (-0.5)
    query_pos = jnp.arange(row_count, dtype=jnp.int32)

    def key_block(state, block_index):
        running, norm_sum, weighted = state
        key_begin = block_index * TOK_DEV
        latent = lax.dynamic_slice_in_dim(latent_kv, key_begin, TOK_DEV, 1).astype(jnp.float32)
        rotary = lax.dynamic_slice_in_dim(key_rope, key_begin, TOK_DEV, 1).astype(jnp.float32)
        scores = jnp.einsum('thl,ls->ths', query_lat, latent) + jnp.einsum('thr,rs->ths', query_rot, rotary)
        scores = scores * score_scale
        key_pos = key_begin + jnp.arange(TOK_DEV, dtype=jnp.int32)
        allowed = (key_pos[None, :] <= query_pos[:, None])[:, None, :]
        new_max = jnp.maximum(running, lax.optimization_barrier(jnp.max(jnp.where(allowed, scores, LOW_SCORE), axis=2)))
        exp_scores = jnp.where(allowed, jnp.exp(scores - new_max[:, :, None]), 0.0)
        factor = jnp.exp(running - new_max)
        norm_sum = norm_sum * factor + lax.optimization_barrier(jnp.sum(exp_scores, axis=2))
        rounded = lax.optimization_barrier(exp_scores.astype(jnp.bfloat16)).astype(jnp.float32)
        weighted = weighted * factor[:, :, None] + jnp.einsum('ths,ls->thl', rounded, latent)
        return ((new_max, norm_sum, weighted), None)
    start_state = (jnp.full((row_count, head_count), LOW_SCORE, jnp.float32), jnp.zeros((row_count, head_count), jnp.float32), jnp.zeros((row_count, head_count, LATENT), jnp.float32))
    final_state, _ = lax.scan(key_block, start_state, jnp.arange(N_CTX, dtype=jnp.int32))
    running, norm_sum, weighted = final_state
    attn_lat = weighted / norm_sum[:, :, None]
    attn_lat = lax.optimization_barrier(attn_lat.astype(jnp.bfloat16)).astype(jnp.float32)
    heads_out = jnp.einsum('thl,hlv->thv', attn_lat, absorb_value.astype(jnp.float32)).astype(jnp.bfloat16)
    attn_sum = jnp.dot(heads_out.reshape(row_count, head_count * VDIM), out_proj, preferred_element_type=jnp.float32)
    residual = x_resid.astype(jnp.float32) + attn_sum
    inv_rms = lax.rsqrt(lax.optimization_barrier(jnp.mean(residual * residual, axis=1)) + EPS)
    normed = residual * inv_rms[:, None] * norm_gain.astype(jnp.float32)[None, :]
    logits = jnp.dot(normed, router.astype(jnp.float32).T, precision=lax.Precision.HIGHEST)
    normed_rows = normed.astype(jnp.bfloat16)
    expert_ids = jnp.arange(EXPERTS, dtype=jnp.int32)
    onehot = routes[:, :, None] == expert_ids[None, None, :]
    chosen = lax.optimization_barrier(jnp.sum(jnp.where(onehot, logits[:, None, :], 0.0), axis=2))
    gate_vals = jax.nn.sigmoid(chosen)
    gate_vals = ROUTE_SCALE * gate_vals / lax.optimization_barrier(jnp.sum(gate_vals, axis=1, keepdims=True))
    hit_flags = onehot.astype(jnp.int32).reshape(N_CTX, TOK_DEV * TOP, EXPERTS)
    before = jnp.cumsum(hit_flags, axis=1).astype(jnp.int32) - hit_flags
    slot_ids = lax.optimization_barrier(jnp.sum(before * hit_flags, axis=2)).astype(jnp.int32).reshape(row_count * TOP)
    sources = jnp.arange(row_count * TOP, dtype=jnp.int32) // (TOK_DEV * TOP)
    places = (routes.reshape(row_count * TOP).astype(jnp.int32) * (N_CTX * CAP) + sources * CAP + slot_ids).astype(jnp.int32)
    buffer = jnp.zeros((EXPERTS * N_CTX * CAP, D), jnp.bfloat16).at[places].set(jnp.repeat(normed_rows, TOP, axis=0))
    buffer = buffer.reshape(EXPERTS, N_CTX * CAP, D)
    group_size = EXP_HID // N_TP

    def one_expert(expert_pack):
        slot_rows, gate_mat, up_mat, down_mat = expert_pack
        gate_part = jnp.dot(slot_rows, gate_mat, preferred_element_type=jnp.float32)
        up_part = jnp.dot(slot_rows, up_mat, preferred_element_type=jnp.float32)
        hidden = (jax.nn.silu(gate_part) * up_part).astype(jnp.bfloat16)
        summed = jnp.zeros((slot_rows.shape[0], D), jnp.float32)
        for group_index in range(N_TP):
            lower = group_index * group_size
            partial_term = jnp.dot(hidden[:, lower:lower + group_size], down_mat[lower:lower + group_size], preferred_element_type=jnp.float32)
            summed = summed + lax.optimization_barrier(partial_term.astype(jnp.bfloat16)).astype(jnp.float32)
        return summed.astype(jnp.bfloat16)
    outputs = lax.map(one_expert, (buffer, gate_proj, up_proj, down_proj))
    picked = outputs.reshape(EXPERTS * N_CTX * CAP, D)[places].reshape(row_count, TOP, D)
    routed_sum = lax.optimization_barrier(jnp.sum(gate_vals[:, :, None] * picked.astype(jnp.float32), axis=1))
    return (residual + routed_sum).astype(jnp.bfloat16)
```

```python
import functools

import jax
import jax.numpy as jnp
from jax import lax
from jax.experimental import pallas as pl
from jax.experimental.pallas import tpu as pltpu
from jax.sharding import PartitionSpec as P

NOPE = 128
ROPE = 64
VDIM = 128
TOP = 4
NZ = 4
NX = 4
NY = 4

EPS = 1e-06
ROUTE_SCALE = 2.5
LOW_SCORE = -1e30
LOG2E = 1.4426950408889634
F32 = jnp.float32
BF16 = jnp.bfloat16
AXES = ("ctx", "tp")


def shift(value, first=(0, 0), second=None, dy=0, dc=0):
    second = first if second is None else second
    pairs = []
    for z in range(NZ):
        for x in range(NX):
            for y in range(NY):
                for c in range(2):
                    dz, dx = second if c else first
                    to_ctx = (z + dz) % NZ * NX + (x + dx) % NX
                    to_tp = (y + dy) % NY * 2 + (c ^ dc)
                    pairs.append(((z * NX + x) * 8 + y * 2 + c, to_ctx * 8 + to_tp))
    return lax.ppermute(value, AXES, pairs)


def dot(a, b, ca=1, cb=0):
    return lax.dot_general(a, b, (((ca,), (cb,)), ((), ())), preferred_element_type=F32)


def attention_kernel(
    place, key_pos, mine, other, q_nope, q_rope, absorb_key, absorb_value, out_proj,
    own_out, core_out, keys, total,
):
    step = pl.program_id(0)
    core, ctx, row_y = place[0], place[1], place[2]
    rows = q_nope.shape[0]
    half = mine.shape[0]
    block = mine.shape[1] // 16

    def put(row0, ref, turned):
        for i in range(16):
            j = i % 4 * 4 + i // 4 if turned else i
            keys[row0 : row0 + half, i * block : (i + 1) * block] = ref[
                :, j * block : (j + 1) * block
            ]

    @pl.when((step == 0) & (core == 0))
    def _():
        put(0, mine, False)
        put(half, other, True)

    @pl.when((step == 0) & (core == 1))
    def _():
        put(0, other, False)
        put(half, mine, True)

    heads = absorb_key.shape[0]
    latent_size = absorb_key.shape[2]
    queries = []
    for h in range(heads):
        lat = dot(q_nope[:, h * NOPE : (h + 1) * NOPE], absorb_key[h]).astype(BF16)
        queries.append(jnp.concatenate([lat, q_rope[:, h * ROPE : (h + 1) * ROPE]], axis=1))
    queries = jnp.concatenate(queries, axis=0)
    scores = dot(queries, keys[...])
    shape = (rows, key_pos.shape[1])
    query_pos = ctx * rows + lax.broadcasted_iota(jnp.int32, shape, 0)
    allowed = jnp.broadcast_to(key_pos[...], shape) <= query_pos
    allowed = jnp.concatenate([allowed] * heads, axis=0)
    scores = jnp.where(allowed, scores, LOW_SCORE)
    top = jnp.max(scores, axis=1, keepdims=True)
    factor = LOG2E * (NOPE + ROPE) ** (-0.5)
    weights = jnp.exp2((scores - top) * factor)
    norm = jnp.sum(weights, axis=1, keepdims=True)
    lat_out = dot(weights.astype(BF16), keys[:latent_size, :], 1, 1)
    lat_out = (lat_out / norm).astype(BF16)
    outs = [
        dot(lat_out[h * rows : (h + 1) * rows], absorb_value[h]).astype(BF16)
        for h in range(heads)
    ]
    part = dot(jnp.concatenate(outs, axis=1), out_proj[...])

    @pl.when(step == 0)
    def _():
        total[...] = part

    @pl.when(step > 0)
    def _():
        total[...] += part

    @pl.when(step == pl.num_programs(0) - 1)
    def _():
        width = own_out.shape[2]
        for d in range(NY):
            chunk = lax.rem(row_y + d, NY) * 2
            own = pl.multiple_of((chunk + core) * width, 128)
            far = pl.multiple_of((chunk + 1 - core) * width, 128)
            own_out[d] = total[:, pl.ds(own, width)]
            core_out[d] = total[:, pl.ds(far, width)].astype(BF16)


def attention(place, key_pos, mine, other, q_nope, q_rope, absorb_key, absorb_value, out_proj):
    rows = q_nope.shape[0]
    head_count = absorb_key.shape[0]
    latent_size = absorb_key.shape[2]
    width = out_proj.shape[1]
    per = 2
    key_count = key_pos.shape[1]
    depth = 2 * mine.shape[0]
    fixed = lambda shape: pl.BlockSpec(shape, lambda i: (0,) * len(shape))
    chunk = (NY, rows, width // (2 * NY))
    return pl.pallas_call(
        attention_kernel,
        grid=(head_count // per,),
        in_specs=[
            pl.BlockSpec(memory_space=pltpu.SMEM),
            fixed(key_pos.shape),
            fixed(mine.shape),
            fixed(other.shape),
            pl.BlockSpec((rows, per * NOPE), lambda i: (0, i)),
            pl.BlockSpec((rows, per * ROPE), lambda i: (0, i)),
            pl.BlockSpec((per,) + absorb_key.shape[1:], lambda i: (i, 0, 0)),
            pl.BlockSpec((per,) + absorb_value.shape[1:], lambda i: (i, 0, 0)),
            pl.BlockSpec((per * VDIM, width), lambda i: (i, 0)),
        ],
        out_specs=[fixed(chunk), fixed(chunk)],
        out_shape=[
            jax.ShapeDtypeStruct(chunk, F32),
            jax.ShapeDtypeStruct(chunk, BF16),
        ],
        scratch_shapes=[
            pltpu.VMEM((depth, key_count), BF16),
            pltpu.VMEM((rows, width), F32),
        ],
        compiler_params=pltpu.CompilerParams(vmem_limit_bytes=50 * 1024 * 1024),
        cost_estimate=pl.CostEstimate(
            flops=2 * rows * head_count * key_count * (depth + latent_size)
            + 2 * rows * head_count * VDIM * width,
            bytes_accessed=out_proj.size * 2 + 4 * mine.size,
            transcendentals=rows * head_count * key_count,
        ),
        name="attention",
    )(place, key_pos, mine, other, q_nope, q_rope, absorb_key, absorb_value, out_proj)


def gate_up_kernel(place, mine, other, weight, inv_gain, own_out, own_square, far_out, square):
    step = pl.program_id(0)
    rows = mine.shape[0]
    depth = mine.shape[1]
    wide = weight.shape[2]
    near = pl.multiple_of(place[0] * depth, 128)
    away = pl.multiple_of((1 - place[0]) * depth, 128)

    @pl.when(step == 0)
    def _():
        ones = jnp.ones((8, depth), BF16)
        held = jnp.zeros((8, rows), F32)
        for start, ref in ((near, mine), (away, other)):
            value = ref[...].astype(F32) * inv_gain[:, pl.ds(start, depth)]
            held = held + dot(ones, (value * value).astype(BF16), 1, 1)
        row = lax.broadcasted_iota(jnp.int32, (8, wide), 0)
        picked = jnp.zeros((8, wide), F32)
        for q in range(rows // wide):
            picked = jnp.where(lax.rem(row, 4) == q, held[:, q * wide : (q + 1) * wide], picked)
        own_square[...] = picked
        high = picked.astype(BF16)
        low = (picked - high.astype(F32)).astype(BF16)
        both = jnp.where(row < 4, high.astype(F32), low.astype(F32))
        square[...] = jnp.concatenate([both, jnp.zeros((8, wide), F32)], axis=0).astype(BF16)

    value = dot(mine[...], weight[0, pl.ds(near, depth), :])
    value = value + dot(other[...], weight[0, pl.ds(away, depth), :])

    @pl.when(step < NY - 1)
    def _():
        far_out[0, :rows, :] = value.astype(BF16)
        far_out[0, rows:, :] = square[...]

    @pl.when(step == NY - 1)
    def _():
        own_out[...] = value


def gate_up(place, mine, other, weight, inv_gain):
    rows, depth = mine.shape
    wide = weight.shape[2]
    fixed = lambda shape: pl.BlockSpec(shape, lambda i: (0,) * len(shape))
    return pl.pallas_call(
        gate_up_kernel,
        grid=(NY,),
        in_specs=[
            pl.BlockSpec(memory_space=pltpu.SMEM),
            fixed(mine.shape),
            fixed(other.shape),
            pl.BlockSpec((1, 2 * depth, wide), lambda i: ((i + 1) % NY, 0, 0)),
            fixed(inv_gain.shape),
        ],
        out_specs=[
            fixed((rows, wide)),
            fixed((8, wide)),
            pl.BlockSpec((1, rows + 16, wide), lambda i: (jnp.minimum(i, NY - 2), 0, 0)),
        ],
        out_shape=[
            jax.ShapeDtypeStruct((rows, wide), F32),
            jax.ShapeDtypeStruct((8, wide), F32),
            jax.ShapeDtypeStruct((NY - 1, rows + 16, wide), BF16),
        ],
        scratch_shapes=[pltpu.VMEM((16, wide), BF16)],
        compiler_params=pltpu.CompilerParams(vmem_limit_bytes=40 * 1024 * 1024),
        cost_estimate=pl.CostEstimate(
            flops=2 * rows * 2 * depth * wide * NY,
            bytes_accessed=4 * mine.size + weight.size * 2,
            transcendentals=0,
        ),
        name="gate_up",
    )(place, mine, other, weight, inv_gain)


def hidden_kernel(full, own, own_square, first, second, third, out):
    rows, wide = own.shape
    far = (first, second, third)
    square = own_square[0:8, :]
    low = jnp.zeros((8, wide), F32)
    for ref in far:
        both = ref[rows : rows + 16, :].astype(F32)
        low = low + both[0:8]
    row = lax.broadcasted_iota(jnp.int32, (8, wide), 0)
    square = jnp.where(row < 4, square, 0.0) + low
    square = square[0:4] + square[4:8]
    scale = lax.rsqrt(square / full + EPS)
    part = wide // 2
    for k in range(rows // part):
        line = scale[k // 2 : k // 2 + 1, k % 2 * part : (k % 2 + 1) * part]
        factor = jnp.transpose(jnp.broadcast_to(line, (part, part)))
        at = slice(k * part, (k + 1) * part)
        value = own[at, :]
        for ref in far:
            value = value + ref[at, :].astype(F32)
        gate = value[:, :part] * factor
        up = value[:, part:] * factor
        out[at, :] = (gate / (1.0 + jnp.exp(-gate)) * up).astype(BF16)


def hidden_of(own, own_square, far, full):
    rows, wide = own.shape
    return pl.pallas_call(
        functools.partial(hidden_kernel, full),
        out_shape=jax.ShapeDtypeStruct((rows, wide // 2), BF16),
        compiler_params=pltpu.CompilerParams(vmem_limit_bytes=32 * 1024 * 1024),
        cost_estimate=pl.CostEstimate(
            flops=8 * rows * wide, bytes_accessed=own.size * 10, transcendentals=rows * wide
        ),
        name="hidden",
    )(own, own_square, *far)


def body(
    x_resid,
    query_nope,
    query_rope,
    latent_kv,
    key_rope,
    absorb_key,
    absorb_value,
    out_proj,
    norm_gain,
    router,
    routes,
    gate_proj,
    up_proj,
    down_proj,
):
    rows, width = x_resid.shape
    experts = lax.axis_size("ctx")
    capacity = 2 * rows * TOP // experts
    full = out_proj.shape[1]
    ctx = lax.axis_index("ctx")
    tp = lax.axis_index("tp")
    core = tp % 2
    row_y = tp // 2
    z, x = ctx // NX, ctx % NX

    with jax.named_scope("key_gather"):
        keys = jnp.concatenate([latent_kv, key_rope], axis=0)
        half = keys.shape[0] // 2
        piece = lax.dynamic_slice_in_dim(keys, core * half, half, 0)
        line = jnp.concatenate(
            [piece] + [shift(piece, (d, 0), (0, d)) for d in range(1, 4)], axis=1
        )
        mine = jnp.concatenate(
            [line] + [shift(line, (0, d), (d, 0)) for d in range(1, 4)], axis=1
        )
        other = shift(mine, dc=1)
        order = jnp.arange(16, dtype=jnp.int32)
        source = (z - order % 4 + 4) % 4 * 4 + (x - order // 4 + 4) % 4
        key_pos = source[:, None] * rows + jnp.arange(rows, dtype=jnp.int32)[None, :]
        key_pos = key_pos.reshape(1, 16 * rows)

    with jax.named_scope("weights_gate_up"):
        cut = []
        for d in range(NY):
            start = (row_y + d) % NY * 2 * width
            block = jnp.concatenate(
                [
                    lax.dynamic_slice_in_dim(gate_proj[0], start, 2 * width, 0),
                    lax.dynamic_slice_in_dim(up_proj[0], start, 2 * width, 0),
                ],
                axis=1,
            )
            cut.append(block if d == 0 else shift(block, dy=d))

    with jax.named_scope("slots"):
        expert_ids = jnp.arange(experts, dtype=jnp.int32)
        named = jnp.any(routes[:, :, None] == expert_ids[None, None, :], axis=1).T
        token = jnp.arange(rows, dtype=jnp.int32)
        earlier = (token[:, None] < token[None, :]).astype(BF16)
        slot = jnp.dot(named.astype(BF16), earlier, preferred_element_type=F32)
        slot = slot.astype(jnp.int32)
        placed = named[:, None, :] & (
            slot[:, None, :] == jnp.arange(capacity, dtype=jnp.int32)[None, :, None]
        )
        placed = placed.astype(BF16).reshape(experts * capacity, rows)

    place = jnp.stack([core, ctx, row_y]).astype(jnp.int32)
    own_part, core_part = attention(
        place, key_pos, mine, other, query_nope, query_rope, absorb_key, absorb_value, out_proj
    )

    own_part, core_part, cut = lax.optimization_barrier((own_part, core_part, cut))
    gate_up_w = jnp.stack(cut)

    with jax.named_scope("attn_sum"):
        pair = own_part + shift(core_part, dc=1).astype(F32)
        pair_low = pair.astype(BF16)
        resid = x_resid.astype(F32) + pair[0]
        for d in range(1, NY):
            resid = resid + shift(pair_low[d], dy=d).astype(F32)

    with jax.named_scope("weights_down"):
        resid, down = lax.optimization_barrier((resid, down_proj[0]))
        own_cut, core_cut = [], []
        for d in range(NY):
            start = (row_y + d) % NY * 2 * width
            block = lax.dynamic_slice_in_dim(down, start, 2 * width, 1)
            block = block if d == 0 else shift(block, dy=d)
            own_cut.append(lax.dynamic_slice_in_dim(block, core * width, width, 1))
            core_cut.append(lax.dynamic_slice_in_dim(block, (1 - core) * width, width, 1))
        own_down = jnp.concatenate(own_cut, axis=0)
        far_down = shift(jnp.concatenate(core_cut, axis=0), dc=1)

    with jax.named_scope("dispatch"):
        col_start = tp * width
        gain = lax.dynamic_slice_in_dim(norm_gain, col_start, width, 0).astype(F32)
        scaled = resid * gain[None, :]
        outgoing = scaled.astype(BF16)
        buffer = jnp.dot(placed, outgoing, preferred_element_type=F32).astype(BF16)
        arrived = lax.all_to_all(
            buffer.reshape(experts, capacity, width), "ctx", split_axis=0, concat_axis=0, tiled=True
        ).reshape(experts * capacity, width)
        arrived, own_down, far_down = lax.optimization_barrier((arrived, own_down, far_down))

    with jax.named_scope("gates"):
        router_cols = lax.dynamic_slice_in_dim(router, col_start, width, 1).astype(F32)
        logits = lax.dot_general(
            router_cols, scaled, (((1,), (1,)), ((), ())), precision=lax.Precision.HIGHEST
        )
        square = jnp.sum(resid * resid, axis=1)[None, :]
        stats = jnp.concatenate([logits, jnp.broadcast_to(square, (8, rows))], axis=0)
        stats = stats + shift(stats, dc=1)
        stats = stats + sum(shift(stats, dy=d) for d in range(1, NY))
        inv_rms = lax.rsqrt(stats[experts] / full + EPS)
        gates = jnp.where(named, jax.nn.sigmoid(stats[:experts] * inv_rms[None, :]), 0.0)
        gates = ROUTE_SCALE * gates / jnp.sum(gates, axis=0, keepdims=True)
        gate_high = gates.astype(BF16)
        gate_low = (gates - gate_high.astype(F32)).astype(BF16)
        spread = placed.reshape(experts, capacity, rows)
        mix_high = (spread * gate_high[:, None, :]).reshape(experts * capacity, rows)
        mix_low = (spread * gate_low[:, None, :]).reshape(experts * capacity, rows)

    with jax.named_scope("experts"):
        far_cols = shift(arrived, dc=1)
        inv_gain = lax.dynamic_slice_in_dim(norm_gain, row_y * 2 * width, 2 * width, 0)
        inv_gain = (1.0 / inv_gain.astype(F32)).reshape(1, 2 * width)
        own, own_square, far = gate_up(place, arrived, far_cols, gate_up_w, inv_gain)
        far = [shift(far[d - 1], dy=-d) for d in range(1, NY)]
        hidden = hidden_of(own, own_square, far, float(full))
        hidden = jnp.concatenate(
            [hidden] + [shift(hidden, dy=d) for d in range(1, NY)], axis=1
        )
        far_hidden = shift(hidden, dc=1)
        result = jnp.dot(hidden, own_down, preferred_element_type=F32) + jnp.dot(
            far_hidden, far_down, preferred_element_type=F32
        )
        result = result.astype(BF16)

    with jax.named_scope("combine"):
        returned = lax.all_to_all(
            result.reshape(experts, capacity, width), "ctx", split_axis=0, concat_axis=0, tiled=True
        ).reshape(experts * capacity, width)
        routed = dot(mix_high, returned, 0, 0) + dot(mix_low, returned, 0, 0)
        return (resid + routed).astype(BF16)


def solution(mesh):
    return jax.shard_map(
        body,
        mesh=mesh,
        in_specs=(
            P("ctx", "tp"),
            P("ctx", "tp"),
            P("ctx", "tp"),
            P(None, "ctx"),
            P(None, "ctx"),
            P("tp", None, None),
            P("tp", None, None),
            P("tp", None),
            P(),
            P(),
            P("ctx", None),
            P("ctx", None, "tp"),
            P("ctx", None, "tp"),
            P("ctx", "tp", None),
        ),
        out_specs=P("ctx", "tp"),
        check_vma=False,
    )
```

```python
import functools

import jax
import jax.numpy as jnp
from jax import lax
from jax.experimental import pallas as pl
from jax.experimental.pallas import tpu as pltpu
from jax.sharding import PartitionSpec as P

NOPE = 128
ROPE = 64
VDIM = 128
TOP = 4
NZ = 4
NX = 4
NY = 4

EPS = 1e-06
ROUTE_SCALE = 2.5
LOW_SCORE = -1e30
LOG2E = 1.4426950408889634
F32 = jnp.float32
BF16 = jnp.bfloat16
AXES = ("ctx", "tp")


def shift(value, first=(0, 0), second=None, dy=0, dc=0):
    second = first if second is None else second
    pairs = []
    for z in range(NZ):
        for x in range(NX):
            for y in range(NY):
                for c in range(2):
                    dz, dx = second if c else first
                    to_ctx = (z + dz) % NZ * NX + (x + dx) % NX
                    to_tp = (y + dy) % NY * 2 + (c ^ dc)
                    pairs.append(((z * NX + x) * 8 + y * 2 + c, to_ctx * 8 + to_tp))
    return lax.ppermute(value, AXES, pairs)


def dot(a, b, ca=1, cb=0):
    return lax.dot_general(a, b, (((ca,), (cb,)), ((), ())), preferred_element_type=F32)


def attention_kernel(
    place, bias, mine, other, q_nope, q_rope, absorb_key, absorb_value, out_proj,
    own_out, core_out, keys, total,
):
    step = pl.program_id(0)
    core, row_y = place[0], place[2]
    rows = q_nope.shape[0]
    half = mine.shape[0]
    block = mine.shape[1] // 16

    def put(row0, ref, turned):
        for i in range(16):
            j = i % 4 * 4 + i // 4 if turned else i
            keys[row0 : row0 + half, i * block : (i + 1) * block] = ref[
                :, j * block : (j + 1) * block
            ]

    @pl.when(step == 0)
    def _():
        keys[2 * half :, :] = bias[...]

    @pl.when((step == 0) & (core == 0))
    def _():
        put(0, mine, False)
        put(half, other, True)

    @pl.when((step == 0) & (core == 1))
    def _():
        put(0, other, False)
        put(half, mine, True)

    heads = absorb_key.shape[0]
    latent_size = absorb_key.shape[2]
    queries = []
    for h in range(heads):
        lat = dot(q_nope[:, h * NOPE : (h + 1) * NOPE], absorb_key[h]).astype(BF16)
        rope = q_rope[:, h * ROPE : (h + 1) * ROPE]
        queries.append(jnp.concatenate([lat, rope, jnp.ones((rows, 16), BF16)], axis=1))
    queries = jnp.concatenate(queries, axis=0)
    scores = dot(queries, keys[...])
    shape = (heads * rows, block)
    query = lax.rem(lax.broadcasted_iota(jnp.int32, shape, 0), rows)
    allowed = lax.broadcasted_iota(jnp.int32, shape, 1) <= query
    own = jnp.where(allowed, scores[:, :block], LOW_SCORE)
    scores = jnp.concatenate([own, scores[:, block:]], axis=1)
    top = jnp.max(scores, axis=1, keepdims=True)
    factor = LOG2E * (NOPE + ROPE) ** (-0.5)
    weights = jnp.exp2((scores - top) * factor)
    norm = jnp.sum(weights, axis=1, keepdims=True)
    lat_out = dot(weights.astype(BF16), keys[:latent_size, :], 1, 1)
    lat_out = (lat_out / norm).astype(BF16)
    outs = [
        dot(lat_out[h * rows : (h + 1) * rows], absorb_value[h]).astype(BF16)
        for h in range(heads)
    ]
    part = dot(jnp.concatenate(outs, axis=1), out_proj[...])

    @pl.when(step == 0)
    def _():
        total[...] = part

    @pl.when(step > 0)
    def _():
        total[...] += part

    @pl.when(step == pl.num_programs(0) - 1)
    def _():
        width = own_out.shape[2]
        for d in range(NY):
            chunk = lax.rem(row_y + d, NY) * 2
            own = pl.multiple_of((chunk + core) * width, 128)
            far = pl.multiple_of((chunk + 1 - core) * width, 128)
            own_out[d] = total[:, pl.ds(own, width)]
            core_out[d] = total[:, pl.ds(far, width)].astype(BF16)


def attention(place, bias, mine, other, q_nope, q_rope, absorb_key, absorb_value, out_proj):
    rows = q_nope.shape[0]
    head_count = absorb_key.shape[0]
    latent_size = absorb_key.shape[2]
    width = out_proj.shape[1]
    per = 4
    key_count = bias.shape[1]
    depth = 2 * mine.shape[0] + bias.shape[0]
    fixed = lambda shape: pl.BlockSpec(shape, lambda i: (0,) * len(shape))
    chunk = (NY, rows, width // (2 * NY))
    return pl.pallas_call(
        attention_kernel,
        grid=(head_count // per,),
        in_specs=[
            pl.BlockSpec(memory_space=pltpu.SMEM),
            fixed(bias.shape),
            fixed(mine.shape),
            fixed(other.shape),
            pl.BlockSpec((rows, per * NOPE), lambda i: (0, i)),
            pl.BlockSpec((rows, per * ROPE), lambda i: (0, i)),
            pl.BlockSpec((per,) + absorb_key.shape[1:], lambda i: (i, 0, 0)),
            pl.BlockSpec((per,) + absorb_value.shape[1:], lambda i: (i, 0, 0)),
            pl.BlockSpec((per * VDIM, width), lambda i: (i, 0)),
        ],
        out_specs=[fixed(chunk), fixed(chunk)],
        out_shape=[
            jax.ShapeDtypeStruct(chunk, F32),
            jax.ShapeDtypeStruct(chunk, BF16),
        ],
        scratch_shapes=[
            pltpu.VMEM((depth, key_count), BF16),
            pltpu.VMEM((rows, width), F32),
        ],
        compiler_params=pltpu.CompilerParams(vmem_limit_bytes=60 * 1024 * 1024),
        cost_estimate=pl.CostEstimate(
            flops=2 * rows * head_count * key_count * (depth + latent_size)
            + 2 * rows * head_count * VDIM * width,
            bytes_accessed=out_proj.size * 2 + 4 * mine.size,
            transcendentals=rows * head_count * key_count,
        ),
        name="attention",
    )(place, bias, mine, other, q_nope, q_rope, absorb_key, absorb_value, out_proj)


FIRST_CUTS = ((1, 0, 1280), (3, 0, 1280))
LATER_CUTS = ((1, 1280, 1792), (3, 1280, 1792), (2, 0, 1344), (2, 1344, 1792))


def cut_kernel(cuts, place, gate, up, down, *rest):
    outs, sems = rest[:-1], rest[-1]
    part = gate.shape[1]
    depth = gate.shape[0] // NY
    copies = []
    for out, (d, first, _) in zip(outs, cuts):
        start = pl.multiple_of(lax.rem(place[2] + d, NY) * depth + first, 64)
        for k, source in enumerate((gate, up)):
            copies.append(
                (source.at[pl.ds(start, out.shape[0]), :], out.at[:, k * part : (k + 1) * part])
            )
    for d, out in enumerate(outs[len(cuts) :]):
        start = pl.multiple_of(lax.rem(place[2] + d + 1, NY) * depth, 128)
        copies.append((down.at[:, pl.ds(start, depth)], out))
    copies = [pltpu.make_async_copy(a, b, sems.at[i]) for i, (a, b) in enumerate(copies)]
    for copy in copies:
        copy.start()
    for copy in copies:
        copy.wait()


def cut_weights(name, cuts, down_count, place, gate, up, down):
    hbm = pl.BlockSpec(memory_space=pltpu.HBM)
    outs = pl.pallas_call(
        functools.partial(cut_kernel, cuts),
        in_specs=[pl.BlockSpec(memory_space=pltpu.SMEM), hbm, hbm, hbm],
        out_shape=[
            jax.ShapeDtypeStruct((end - first, 2 * gate.shape[1]), BF16) for _, first, end in cuts
        ]
        + [jax.ShapeDtypeStruct((down.shape[0], down.shape[1] // NY), BF16)] * down_count,
        scratch_shapes=[pltpu.SemaphoreType.DMA((2 * len(cuts) + down_count,))],
        compiler_params=pltpu.CompilerParams(vmem_limit_bytes=60 * 1024 * 1024),
        cost_estimate=pl.CostEstimate(
            flops=0, bytes_accessed=4 * gate.size, transcendentals=0
        ),
        name=name,
    )(place, gate, up, down)
    return outs[: len(cuts)], outs[len(cuts) :]


def unpack_kernel(place, first, second, third, down, own, far, kept, sem):
    rows, depth = kept.shape
    width = depth // 2
    start = pl.multiple_of(place[2] * depth, 128)
    copy = pltpu.make_async_copy(down.at[:, pl.ds(start, depth)], kept, sem)
    copy.start()
    near = pl.multiple_of(place[0] * width, 128)
    away = pl.multiple_of((1 - place[0]) * width, 128)
    for d, ref in ((1, first), (2, second), (3, third), (0, kept)):
        if d == 0:
            copy.wait()
        own[d * rows : (d + 1) * rows, :] = ref[:, pl.ds(near, width)]
        far[d * rows : (d + 1) * rows, :] = ref[:, pl.ds(away, width)]


def unpack(place, moved, down):
    rows, depth = moved[0].shape
    vmem = pl.BlockSpec(memory_space=pltpu.VMEM)
    return pl.pallas_call(
        unpack_kernel,
        in_specs=[pl.BlockSpec(memory_space=pltpu.SMEM), vmem, vmem, vmem]
        + [pl.BlockSpec(memory_space=pltpu.HBM)],
        out_shape=[jax.ShapeDtypeStruct((NY * rows, depth // 2), BF16)] * 2,
        scratch_shapes=[pltpu.VMEM((rows, depth), BF16), pltpu.SemaphoreType.DMA],
        compiler_params=pltpu.CompilerParams(vmem_limit_bytes=12 * 1024 * 1024),
        cost_estimate=pl.CostEstimate(
            flops=0, bytes_accessed=16 * rows * depth, transcendentals=0
        ),
        name="unpack",
    )(place, *moved, down)


def slots_of(line, capacity):
    ids = lax.broadcasted_iota(jnp.int32, (capacity, line.shape[1]), 0)
    return jnp.broadcast_to(line, ids.shape) == ids


def fill_kernel(slot, t0, t1, t2, t3, *outs):
    for e, out in enumerate(outs):
        capacity = out.shape[0] // NY
        for d, ref in enumerate((t0, t1, t2, t3)):
            at = d * 4 + e
            placed = slots_of(slot[at : at + 1, :], capacity).astype(BF16)
            out[d * capacity : (d + 1) * capacity, :] = dot(placed, ref[...]).astype(BF16)


def fill(slot, tokens, capacity):
    rows, width = tokens[0].shape
    return pl.pallas_call(
        fill_kernel,
        out_shape=[jax.ShapeDtypeStruct((4 * capacity, width), BF16)] * 4,
        compiler_params=pltpu.CompilerParams(vmem_limit_bytes=16 * 1024 * 1024),
        cost_estimate=pl.CostEstimate(
            flops=32 * capacity * rows * width,
            bytes_accessed=8 * rows * width + 32 * capacity * width,
            transcendentals=0,
        ),
        name="fill",
    )(slot, *tokens)


def mix_kernel(slot, gates, r0, r1, r2, r3, own, *far):
    capacity = r0.shape[0] // 4
    for d in range(4):
        high, low, rows = [], [], []
        for e, ref in enumerate((r0, r1, r2, r3)):
            at = d * 4 + e
            placed = slots_of(slot[at : at + 1, :], capacity)
            value = jnp.where(placed, jnp.broadcast_to(gates[at : at + 1, :], placed.shape), 0.0)
            first = value.astype(BF16)
            high.append(first)
            low.append((value - first.astype(F32)).astype(BF16))
            rows.append(ref[d * capacity : (d + 1) * capacity, :])
        rows = jnp.concatenate(rows, axis=0)
        total = dot(jnp.concatenate(high, axis=0), rows, 0, 0)
        total = total + dot(jnp.concatenate(low, axis=0), rows, 0, 0)
        if d == 0:
            own[...] = total
        else:
            far[d - 1][...] = total.astype(BF16)


def mix(slot, gates, returned):
    width = returned[0].shape[1]
    rows = slot.shape[1]
    return pl.pallas_call(
        mix_kernel,
        out_shape=[jax.ShapeDtypeStruct((rows, width), F32)]
        + [jax.ShapeDtypeStruct((rows, width), BF16)] * 3,
        compiler_params=pltpu.CompilerParams(vmem_limit_bytes=16 * 1024 * 1024),
        cost_estimate=pl.CostEstimate(
            flops=16 * returned[0].size * rows,
            bytes_accessed=8 * returned[0].size + 10 * rows * width,
            transcendentals=0,
        ),
        name="mix",
    )(slot, gates, *returned)


def gather_rows(place, held, mine, other):
    depth = mine[0].shape[1]
    block = mine[0].shape[0] // 4
    near = pl.multiple_of(place[0] * depth, 128)
    away = pl.multiple_of((1 - place[0]) * depth, 128)
    for e in range(4):
        for d in range(4):
            at = (e * 4 + d) * block
            held[at : at + block, pl.ds(near, depth)] = mine[e][d * block : (d + 1) * block, :]
            held[at : at + block, pl.ds(away, depth)] = other[d][e * block : (e + 1) * block, :]


def dot_parts(held, parts):
    total, start = 0.0, 0
    for part in parts:
        total = total + dot(held[:, start : start + part.shape[0]], part[...])
        start += part.shape[0]
    return total


def gate_up_kernel(place, *refs):
    mine, other, parts, inv_gain, stats = refs[:4], refs[4:8], refs[8:14], refs[14], refs[15]
    far_outs, own_square, held = refs[16:19], refs[19], refs[20]
    rows, depth = held.shape
    wide = own_square.shape[1]
    gather_rows(place, held, mine, other)
    row = lax.broadcasted_iota(jnp.int32, (8, wide), 0)
    picked = jnp.zeros((8, wide), F32)
    for q in range(rows // wide):
        lines = []
        for k in range(wide // 128):
            at = q * wide + k * 128
            sums = jnp.zeros((128, 128), F32)
            for c in range(0, depth, 128):
                value = held[at : at + 128, c : c + 128].astype(F32) * inv_gain[:, c : c + 128]
                sums = sums + value * value
            lines.append(jnp.sum(jnp.transpose(sums), axis=0, keepdims=True))
        line = jnp.broadcast_to(jnp.concatenate(lines, axis=1), (8, wide))
        picked = jnp.where(lax.rem(row, 4) == q, line, picked)
    own_square[...] = picked
    high = picked.astype(BF16)
    low = (picked - high.astype(F32)).astype(BF16)
    both = jnp.where(row < 4, high.astype(F32), low.astype(F32))
    high = stats[...].astype(BF16).astype(F32)
    pair = jnp.concatenate([high, stats[...] - high], axis=1)
    both = jnp.concatenate([both, pair], axis=0).astype(BF16)
    for d in range(1, NY):
        out = far_outs[d - 1]
        out[:rows, :] = dot_parts(held, parts[2 * d - 2 : 2 * d]).astype(BF16)
        out[rows:, :] = both


def gate_up(place, mine, other, parts, inv_gain, stats):
    rows, depth = 4 * mine[0].shape[0], 2 * mine[0].shape[1]
    wide = parts[0].shape[1]
    vmem = pl.BlockSpec(memory_space=pltpu.VMEM)
    return pl.pallas_call(
        gate_up_kernel,
        in_specs=[pl.BlockSpec(memory_space=pltpu.SMEM)] + [vmem] * 16,
        out_shape=[jax.ShapeDtypeStruct((rows + 32, wide), BF16)] * 3
        + [jax.ShapeDtypeStruct((8, wide), F32)],
        scratch_shapes=[pltpu.VMEM((rows, depth), BF16)],
        compiler_params=pltpu.CompilerParams(vmem_limit_bytes=60 * 1024 * 1024),
        cost_estimate=pl.CostEstimate(
            flops=8 * rows * depth * wide, bytes_accessed=4 * rows * depth, transcendentals=0
        ),
        name="gate_up",
    )(place, *mine, *other, *parts, inv_gain, stats)


def gate_up_own_kernel(place, *refs):
    mine, other, (gate, up, out, held, weight, sems) = refs[:4], refs[4:8], refs[8:]
    depth = weight.shape[0]
    part = gate.shape[1]
    start = pl.multiple_of(place[2] * depth, 128)
    copies = [
        pltpu.make_async_copy(
            source.at[pl.ds(start, depth), :],
            weight.at[:, k * part : (k + 1) * part],
            sems.at[k],
        )
        for k, source in enumerate((gate, up))
    ]
    for copy in copies:
        copy.start()
    gather_rows(place, held, mine, other)
    for copy in copies:
        copy.wait()
    out[...] = dot(held[...], weight[...])


def gate_up_own(place, mine, other, gate, up):
    rows, depth = 4 * mine[0].shape[0], 2 * mine[0].shape[1]
    wide = 2 * gate.shape[1]
    vmem = pl.BlockSpec(memory_space=pltpu.VMEM)
    hbm = pl.BlockSpec(memory_space=pltpu.HBM)
    return pl.pallas_call(
        gate_up_own_kernel,
        in_specs=[pl.BlockSpec(memory_space=pltpu.SMEM)] + [vmem] * 8 + [hbm] * 2,
        out_shape=jax.ShapeDtypeStruct((rows, wide), F32),
        scratch_shapes=[
            pltpu.VMEM((rows, depth), BF16),
            pltpu.VMEM((depth, wide), BF16),
            pltpu.SemaphoreType.DMA((2,)),
        ],
        compiler_params=pltpu.CompilerParams(vmem_limit_bytes=24 * 1024 * 1024),
        cost_estimate=pl.CostEstimate(
            flops=40 * rows * depth * wide, bytes_accessed=4 * rows * depth, transcendentals=0
        ),
        name="own_part",
    )(place, *mine, *other, gate, up)


def down_kernel(mine, other, own_down, far_down, o0, o1, o2, o3, turned):
    block = o0.shape[0] // 4
    for e in range(4):
        for d in range(4):
            turned[(e * 4 + d) * block : (e * 4 + d + 1) * block, :] = other[
                (d * 4 + e) * block : (d * 4 + e + 1) * block, :
            ]
    for e, out in enumerate((o0, o1, o2, o3)):
        at = slice(e * 4 * block, (e + 1) * 4 * block)
        value = dot(mine[at, :], own_down[...]) + dot(turned[at, :], far_down[...])
        out[...] = value.astype(BF16)


def down(mine, other, own_down, far_down):
    rows, depth = mine.shape
    width = own_down.shape[1]
    return pl.pallas_call(
        down_kernel,
        out_shape=[jax.ShapeDtypeStruct((rows // 4, width), BF16)] * 4,
        scratch_shapes=[pltpu.VMEM((rows, depth), BF16)],
        compiler_params=pltpu.CompilerParams(vmem_limit_bytes=16 * 1024 * 1024),
        cost_estimate=pl.CostEstimate(
            flops=4 * rows * depth * width,
            bytes_accessed=4 * rows * depth + 6 * rows * width,
            transcendentals=0,
        ),
        name="down",
    )(mine, other, own_down, far_down)


def hidden_kernel(full, own, own_square, stats, first, second, third, out, summed):
    rows, wide = own.shape
    far = (first, second, third)
    square = own_square[0:8, :]
    low = jnp.zeros((8, wide), F32)
    total = stats[...]
    for ref in far:
        both = ref[rows : rows + 32, :].astype(F32)
        low = low + both[0:8]
        total = total + both[8:32, :128] + both[8:32, 128:]
    summed[...] = total
    row = lax.broadcasted_iota(jnp.int32, (8, wide), 0)
    square = jnp.where(row < 4, square, 0.0) + low
    square = square[0:4] + square[4:8]
    scale = lax.rsqrt(square / full + EPS)
    part = wide // 2
    for k in range(rows // part):
        line = scale[k // 2 : k // 2 + 1, k % 2 * part : (k % 2 + 1) * part]
        factor = jnp.transpose(jnp.broadcast_to(line, (part, part)))
        at = slice(k * part, (k + 1) * part)
        value = own[at, :]
        for ref in far:
            value = value + ref[at, :].astype(F32)
        gate = value[:, :part] * factor
        up = value[:, part:] * factor
        out[at, :] = (gate / (1.0 + jnp.exp(-gate)) * up).astype(BF16)


def hidden_of(own, own_square, stats, far, full):
    rows, wide = own.shape
    return pl.pallas_call(
        functools.partial(hidden_kernel, full),
        out_shape=[
            jax.ShapeDtypeStruct((rows, wide // 2), BF16),
            jax.ShapeDtypeStruct(stats.shape, F32),
        ],
        compiler_params=pltpu.CompilerParams(vmem_limit_bytes=12 * 1024 * 1024),
        cost_estimate=pl.CostEstimate(
            flops=8 * rows * wide, bytes_accessed=own.size * 10, transcendentals=rows * wide
        ),
        name="hidden",
    )(own, own_square, stats, *far)


def body(
    x_resid,
    query_nope,
    query_rope,
    latent_kv,
    key_rope,
    absorb_key,
    absorb_value,
    out_proj,
    norm_gain,
    router,
    routes,
    gate_proj,
    up_proj,
    down_proj,
):
    rows, width = x_resid.shape
    experts = lax.axis_size("ctx")
    capacity = 2 * rows * TOP // experts
    full = out_proj.shape[1]
    ctx = lax.axis_index("ctx")
    tp = lax.axis_index("tp")
    core = tp % 2
    row_y = tp // 2
    z, x = ctx // NX, ctx % NX

    place = jnp.stack([core, ctx, row_y]).astype(jnp.int32)

    with jax.named_scope("key_gather"):
        expert_ids = jnp.arange(experts, dtype=jnp.int32)
        named = jnp.any(routes[:, :, None] == expert_ids[None, None, :], axis=1).T
        half = (latent_kv.shape[0] + key_rope.shape[0]) // 2
        upper = jnp.concatenate([latent_kv[half:], key_rope], axis=0)
        piece = jnp.where(core == 0, latent_kv[:half], upper)
        piece = jnp.concatenate([piece, named.astype(BF16)], axis=0)
        pieces = [piece] + [shift(piece, (d, 0), (0, d)) for d in range(1, 4)]
        line = jnp.concatenate([p[:half] for p in pieces], axis=1)
        masks = jnp.stack([p[half:] for p in pieces])

    with jax.named_scope("weights_gate_up"):
        weights = (gate_proj[0], up_proj[0], down_proj[0])
        cuts, _ = cut_weights("cut_first", FIRST_CUTS, 0, place, *weights)
        line, cuts = lax.optimization_barrier((line, cuts))
        first0 = shift(cuts[0], dy=1)
        third0 = shift(cuts[1], dy=3)
        line, weights = lax.optimization_barrier((line, weights))
        cuts, down_cuts = cut_weights("cut_later", LATER_CUTS, 3, place, *weights)

    with jax.named_scope("key_gather"):
        mine = jnp.concatenate(
            [line] + [shift(line, (0, d), (d, 0)) for d in range(1, 4)], axis=1
        )
        mine, first0, third0, cuts, down_cuts = lax.optimization_barrier(
            (mine, first0, third0, cuts, down_cuts)
        )
        other = shift(mine, dc=1)
        order = jnp.arange(16, dtype=jnp.int32)
        source = (z - order % 4 + 4) % 4 * 4 + (x - order // 4 + 4) % 4
        bias = jnp.where(source <= ctx, 0.0, LOW_SCORE)[None, :, None]
        bias = jnp.where(order[:, None, None] == 0, bias, 0.0)
        bias = jnp.broadcast_to(bias, (16, 16, rows)).reshape(16, 16 * rows).astype(BF16)

    with jax.named_scope("slots"):
        token = jnp.arange(rows, dtype=jnp.int32)
        earlier = (token[:, None] < token[None, :]).astype(BF16)
        slot = jnp.dot(
            masks.reshape(4 * experts, rows), earlier, preferred_element_type=F32
        ).reshape(4, experts, rows)
        slot = jnp.where(masks > 0, slot, -1.0)
        step = jnp.arange(4, dtype=jnp.int32)
        passing = jnp.where(core == 0, z * NX + (x + step) % NX, (z + step) % NZ * NX + x)
        passing = passing[None, :, None, None] == expert_ids[None, None, :, None]

        def pick(values):
            values = jnp.where(passing, values[:, None], 0.0)
            return jnp.sum(values, axis=2).reshape(16, rows)

        slot = pick(slot).astype(jnp.int32)

    with jax.named_scope("weights_gate_up"):
        first1, third1 = shift(cuts[0], dy=1), shift(cuts[1], dy=3)
        second0 = shift(cuts[2], dy=2)

    own_part, core_part = attention(
        place, bias, mine, other, query_nope, query_rope, absorb_key, absorb_value, out_proj
    )

    own_part, core_part, first1, third1, second0 = lax.optimization_barrier(
        (own_part, core_part, first1, third1, second0)
    )

    with jax.named_scope("attn_sum"):
        pair = own_part + shift(core_part, dc=1).astype(F32)
        pair_low = pair.astype(BF16)
        resid = x_resid.astype(F32) + pair[0]
        for d in range(1, NY):
            resid = resid + shift(pair_low[d], dy=d).astype(F32)

    with jax.named_scope("dispatch"):
        col_start = tp * width
        gain = lax.dynamic_slice_in_dim(norm_gain, col_start, width, 0).astype(F32)
        scaled = resid * gain[None, :]
        outgoing = scaled.astype(BF16)
        router_cols = lax.dynamic_slice_in_dim(router, col_start, width, 1).astype(F32)
        outgoing, late_down, late = lax.optimization_barrier((outgoing, down_cuts, cuts[3]))
        tokens = [outgoing] + [shift(outgoing, (d, 0), (0, d)) for d in range(1, 4)]

    with jax.named_scope("weights_down"):
        moved = [shift(late_down[0], dy=1), None, shift(late_down[2], dy=3)]
        tokens, moved, late, far_cut = lax.optimization_barrier(
            (tokens, moved, late, late_down[1])
        )
        moved[1] = shift(far_cut, dy=2)
        second1 = shift(late, dy=2)

    with jax.named_scope("dispatch"):
        filled = fill(slot, tokens, capacity)
        arrived = [filled[0]] + [shift(filled[e], (0, e), (e, 0)) for e in range(1, 4)]
        arrived, moved[1], second1 = lax.optimization_barrier((arrived, moved[1], second1))
        far_cols = [shift(block, dc=1) for block in arrived]

    with jax.named_scope("gates"):
        scaled, resid_late = lax.optimization_barrier((scaled, resid))
        logits = lax.dot_general(
            router_cols, scaled, (((1,), (1,)), ((), ())), precision=lax.Precision.HIGHEST
        )
        squares = jnp.sum(resid_late * resid_late, axis=1)[None, :]
        stats = jnp.concatenate([logits, jnp.broadcast_to(squares, (8, rows))], axis=0)
        stats = stats + shift(stats, dc=1)

    with jax.named_scope("experts"):
        inv_gain = lax.dynamic_slice_in_dim(norm_gain, row_y * 2 * width, 2 * width, 0)
        inv_gain = (1.0 / inv_gain.astype(F32)).reshape(1, 2 * width)
        parts = (first0, first1, second0, second1, third0, third1)
        *far, own_square = gate_up(place, arrived, far_cols, parts, inv_gain, stats)
        moved, arrived, own_square = lax.optimization_barrier((moved, arrived, own_square))
        far = [shift(far[d - 1], dy=-d) for d in range(1, NY)]
        own = gate_up_own(place, arrived, far_cols, gate_proj[0], up_proj[0])

    with jax.named_scope("weights_down"):
        own_down, far_down = unpack(place, moved, down_proj[0])
        far_down = shift(far_down, dc=1)
        own, own_down, far_down = lax.optimization_barrier((own, own_down, far_down))

    with jax.named_scope("experts"):
        hidden, summed = hidden_of(own, own_square, stats, far, float(full))
        hidden = jnp.concatenate(
            [hidden] + [shift(hidden, dy=d) for d in range(1, NY)], axis=1
        )

    with jax.named_scope("gates"):
        inv_rms = lax.rsqrt(summed[experts] / full + EPS)
        gates = jnp.where(named, jax.nn.sigmoid(summed[:experts] * inv_rms[None, :]), 0.0)
        gates = ROUTE_SCALE * gates / jnp.sum(gates, axis=0, keepdims=True)
        gates = [gates] + [shift(gates, (d, 0), (0, d)) for d in range(1, 4)]
        hidden, gates = lax.optimization_barrier((hidden, gates))
        gates = pick(jnp.stack(gates))

    with jax.named_scope("experts"):
        far_hidden = shift(hidden, dc=1)
        result = down(hidden, far_hidden, own_down, far_down)

    with jax.named_scope("combine"):
        result = [result[0]] + [shift(result[e], (0, -e), (-e, 0)) for e in range(1, 4)]
        own_sum, *far_sum = mix(slot, gates, result)
        total = resid + own_sum
        for d in range(1, 4):
            total = total + shift(far_sum[d - 1], (-d, 0), (0, -d)).astype(F32)
        return total.astype(BF16)


def solution(mesh):
    return jax.shard_map(
        body,
        mesh=mesh,
        in_specs=(
            P("ctx", "tp"),
            P("ctx", "tp"),
            P("ctx", "tp"),
            P(None, "ctx"),
            P(None, "ctx"),
            P("tp", None, None),
            P("tp", None, None),
            P("tp", None),
            P(),
            P(),
            P("ctx", None),
            P("ctx", None, "tp"),
            P("ctx", None, "tp"),
            P("ctx", "tp", None),
        ),
        out_specs=P("ctx", "tp"),
        check_vma=False,
    )
```

```python
import functools

import jax
import jax.numpy as jnp
from jax import lax
from jax.experimental import pallas as pl
from jax.experimental.pallas import tpu as pltpu
from jax.sharding import PartitionSpec as P

NOPE = 128
ROPE = 64
VDIM = 128
TOP = 4
NZ = 4
NX = 4
NY = 4

EPS = 1e-06
ROUTE_SCALE = 2.5
LOW_SCORE = -1e30
LOG2E = 1.4426950408889634
F32 = jnp.float32
BF16 = jnp.bfloat16
AXES = ("ctx", "tp")


def shift(value, first=(0, 0), second=None, dy=0, dc=0):
    second = first if second is None else second
    pairs = []
    for z in range(NZ):
        for x in range(NX):
            for y in range(NY):
                for c in range(2):
                    dz, dx = second if c else first
                    to_ctx = (z + dz) % NZ * NX + (x + dx) % NX
                    to_tp = (y + dy) % NY * 2 + (c ^ dc)
                    pairs.append(((z * NX + x) * 8 + y * 2 + c, to_ctx * 8 + to_tp))
    return lax.ppermute(value, AXES, pairs)


def dot(a, b, ca=1, cb=0):
    return lax.dot_general(a, b, (((ca,), (cb,)), ((), ())), preferred_element_type=F32)


def attention_kernel(
    place, bias, mine, other, q_nope, q_rope, absorb_key, absorb_value, out_proj,
    own_out, core_out, keys, total,
):
    step = pl.program_id(0)
    core, row_y = place[0], place[2]
    rows = q_nope.shape[0]
    half = mine.shape[0]
    block = mine.shape[1] // 16

    def put(row0, ref, turned):
        for i in range(16):
            j = i % 4 * 4 + i // 4 if turned else i
            keys[row0 : row0 + half, i * block : (i + 1) * block] = ref[
                :, j * block : (j + 1) * block
            ]

    @pl.when(step == 0)
    def _():
        keys[2 * half :, :] = bias[...]

    @pl.when((step == 0) & (core == 0))
    def _():
        put(0, mine, False)
        put(half, other, True)

    @pl.when((step == 0) & (core == 1))
    def _():
        put(0, other, False)
        put(half, mine, True)

    heads = absorb_key.shape[0]
    latent_size = absorb_key.shape[2]
    queries = []
    for h in range(heads):
        lat = dot(q_nope[:, h * NOPE : (h + 1) * NOPE], absorb_key[h]).astype(BF16)
        rope = q_rope[:, h * ROPE : (h + 1) * ROPE]
        queries.append(jnp.concatenate([lat, rope, jnp.ones((rows, 16), BF16)], axis=1))
    queries = jnp.concatenate(queries, axis=0)
    scores = dot(queries, keys[...])
    shape = (heads * rows, block)
    query = lax.rem(lax.broadcasted_iota(jnp.int32, shape, 0), rows)
    allowed = lax.broadcasted_iota(jnp.int32, shape, 1) <= query
    own = jnp.where(allowed, scores[:, :block], LOW_SCORE)
    scores = jnp.concatenate([own, scores[:, block:]], axis=1)
    top = jnp.max(scores, axis=1, keepdims=True)
    factor = LOG2E * (NOPE + ROPE) ** (-0.5)
    weights = jnp.exp2((scores - top) * factor)
    norm = jnp.sum(weights, axis=1, keepdims=True)
    lat_out = dot(weights.astype(BF16), keys[:latent_size, :], 1, 1)
    lat_out = (lat_out / norm).astype(BF16)
    outs = [
        dot(lat_out[h * rows : (h + 1) * rows], absorb_value[h]).astype(BF16)
        for h in range(heads)
    ]
    part = dot(jnp.concatenate(outs, axis=1), out_proj[...])

    @pl.when(step == 0)
    def _():
        total[...] = part

    @pl.when(step > 0)
    def _():
        total[...] += part

    @pl.when(step == pl.num_programs(0) - 1)
    def _():
        width = own_out.shape[2]
        for d in range(NY):
            chunk = lax.rem(row_y + d, NY) * 2
            own = pl.multiple_of((chunk + core) * width, 128)
            far = pl.multiple_of((chunk + 1 - core) * width, 128)
            own_out[d] = total[:, pl.ds(own, width)]
            core_out[d] = total[:, pl.ds(far, width)].astype(BF16)


def attention(place, bias, mine, other, q_nope, q_rope, absorb_key, absorb_value, out_proj):
    rows = q_nope.shape[0]
    head_count = absorb_key.shape[0]
    latent_size = absorb_key.shape[2]
    width = out_proj.shape[1]
    per = 4
    key_count = bias.shape[1]
    depth = 2 * mine.shape[0] + bias.shape[0]
    fixed = lambda shape: pl.BlockSpec(shape, lambda i: (0,) * len(shape))
    chunk = (NY, rows, width // (2 * NY))
    return pl.pallas_call(
        attention_kernel,
        grid=(head_count // per,),
        in_specs=[
            pl.BlockSpec(memory_space=pltpu.SMEM),
            fixed(bias.shape),
            fixed(mine.shape),
            fixed(other.shape),
            pl.BlockSpec((rows, per * NOPE), lambda i: (0, i)),
            pl.BlockSpec((rows, per * ROPE), lambda i: (0, i)),
            pl.BlockSpec((per,) + absorb_key.shape[1:], lambda i: (i, 0, 0)),
            pl.BlockSpec((per,) + absorb_value.shape[1:], lambda i: (i, 0, 0)),
            pl.BlockSpec((per * VDIM, width), lambda i: (i, 0)),
        ],
        out_specs=[fixed(chunk), fixed(chunk)],
        out_shape=[
            jax.ShapeDtypeStruct(chunk, F32),
            jax.ShapeDtypeStruct(chunk, BF16),
        ],
        scratch_shapes=[
            pltpu.VMEM((depth, key_count), BF16),
            pltpu.VMEM((rows, width), F32),
        ],
        compiler_params=pltpu.CompilerParams(vmem_limit_bytes=60 * 1024 * 1024),
        cost_estimate=pl.CostEstimate(
            flops=2 * rows * head_count * key_count * (depth + latent_size)
            + 2 * rows * head_count * VDIM * width,
            bytes_accessed=out_proj.size * 2 + 4 * mine.size,
            transcendentals=rows * head_count * key_count,
        ),
        name="attention",
    )(place, bias, mine, other, q_nope, q_rope, absorb_key, absorb_value, out_proj)


FIRST_CUTS = ((1, 0, 1792), (3, 0, 1792))
LATER_CUTS = ((2, 0, 1344), (2, 1344, 1792))


def cut_kernel(cuts, place, gate, up, down, *rest):
    outs, sems = rest[:-1], rest[-1]
    part = gate.shape[1]
    depth = gate.shape[0] // NY
    copies = []
    for out, (d, first, _) in zip(outs, cuts):
        start = pl.multiple_of(lax.rem(place[2] + d, NY) * depth + first, 64)
        for k, source in enumerate((gate, up)):
            copies.append(
                (source.at[pl.ds(start, out.shape[0]), :], out.at[:, k * part : (k + 1) * part])
            )
    for d, out in enumerate(outs[len(cuts) :]):
        start = pl.multiple_of(lax.rem(place[2] + d + 1, NY) * depth, 128)
        copies.append((down.at[:, pl.ds(start, depth)], out))
    copies = [pltpu.make_async_copy(a, b, sems.at[i]) for i, (a, b) in enumerate(copies)]
    for copy in copies:
        copy.start()
    for copy in copies:
        copy.wait()


def cut_weights(name, cuts, down_count, place, gate, up, down):
    hbm = pl.BlockSpec(memory_space=pltpu.HBM)
    outs = pl.pallas_call(
        functools.partial(cut_kernel, cuts),
        in_specs=[pl.BlockSpec(memory_space=pltpu.SMEM), hbm, hbm, hbm],
        out_shape=[
            jax.ShapeDtypeStruct((end - first, 2 * gate.shape[1]), BF16) for _, first, end in cuts
        ]
        + [jax.ShapeDtypeStruct((down.shape[0], down.shape[1] // NY), BF16)] * down_count,
        scratch_shapes=[pltpu.SemaphoreType.DMA((2 * len(cuts) + down_count,))],
        compiler_params=pltpu.CompilerParams(vmem_limit_bytes=60 * 1024 * 1024),
        cost_estimate=pl.CostEstimate(
            flops=0, bytes_accessed=4 * gate.size, transcendentals=0
        ),
        name=name,
    )(place, gate, up, down)
    return outs[: len(cuts)], outs[len(cuts) :]


def unpack_kernel(place, first, second, third, down, own, far, kept, sem):
    rows, depth = kept.shape
    width = depth // 2
    start = pl.multiple_of(place[2] * depth, 128)
    copy = pltpu.make_async_copy(down.at[:, pl.ds(start, depth)], kept, sem)
    copy.start()
    near = pl.multiple_of(place[0] * width, 128)
    away = pl.multiple_of((1 - place[0]) * width, 128)
    for d, ref in ((1, first), (2, second), (3, third), (0, kept)):
        if d == 0:
            copy.wait()
        own[d * rows : (d + 1) * rows, :] = ref[:, pl.ds(near, width)]
        far[d * rows : (d + 1) * rows, :] = ref[:, pl.ds(away, width)]


def unpack(place, moved, down):
    rows, depth = moved[0].shape
    vmem = pl.BlockSpec(memory_space=pltpu.VMEM)
    return pl.pallas_call(
        unpack_kernel,
        in_specs=[pl.BlockSpec(memory_space=pltpu.SMEM), vmem, vmem, vmem]
        + [pl.BlockSpec(memory_space=pltpu.HBM)],
        out_shape=[jax.ShapeDtypeStruct((NY * rows, depth // 2), BF16)] * 2,
        scratch_shapes=[pltpu.VMEM((rows, depth), BF16), pltpu.SemaphoreType.DMA],
        compiler_params=pltpu.CompilerParams(vmem_limit_bytes=12 * 1024 * 1024),
        cost_estimate=pl.CostEstimate(
            flops=0, bytes_accessed=16 * rows * depth, transcendentals=0
        ),
        name="unpack",
    )(place, *moved, down)


def slots_of(line, capacity):
    ids = lax.broadcasted_iota(jnp.int32, (capacity, line.shape[1]), 0)
    return jnp.broadcast_to(line, ids.shape) == ids


def fill_kernel(slot, t0, t1, t2, t3, *outs):
    for e, out in enumerate(outs):
        capacity = out.shape[0] // NY
        for d, ref in enumerate((t0, t1, t2, t3)):
            at = d * 4 + e
            placed = slots_of(slot[at : at + 1, :], capacity).astype(BF16)
            out[d * capacity : (d + 1) * capacity, :] = dot(placed, ref[...]).astype(BF16)


def fill(slot, tokens, capacity):
    rows, width = tokens[0].shape
    return pl.pallas_call(
        fill_kernel,
        out_shape=[jax.ShapeDtypeStruct((4 * capacity, width), BF16)] * 4,
        compiler_params=pltpu.CompilerParams(vmem_limit_bytes=16 * 1024 * 1024),
        cost_estimate=pl.CostEstimate(
            flops=32 * capacity * rows * width,
            bytes_accessed=8 * rows * width + 32 * capacity * width,
            transcendentals=0,
        ),
        name="fill",
    )(slot, *tokens)


def mix_kernel(slot, gates, r0, r1, r2, r3, own, *far):
    capacity = r0.shape[0] // 4
    for d in range(4):
        high, low, rows = [], [], []
        for e, ref in enumerate((r0, r1, r2, r3)):
            at = d * 4 + e
            placed = slots_of(slot[at : at + 1, :], capacity)
            value = jnp.where(placed, jnp.broadcast_to(gates[at : at + 1, :], placed.shape), 0.0)
            first = value.astype(BF16)
            high.append(first)
            low.append((value - first.astype(F32)).astype(BF16))
            rows.append(ref[d * capacity : (d + 1) * capacity, :])
        rows = jnp.concatenate(rows, axis=0)
        total = dot(jnp.concatenate(high, axis=0), rows, 0, 0)
        total = total + dot(jnp.concatenate(low, axis=0), rows, 0, 0)
        if d == 0:
            own[...] = total
        else:
            far[d - 1][...] = total.astype(BF16)


def mix(slot, gates, returned):
    width = returned[0].shape[1]
    rows = slot.shape[1]
    return pl.pallas_call(
        mix_kernel,
        out_shape=[jax.ShapeDtypeStruct((rows, width), F32)]
        + [jax.ShapeDtypeStruct((rows, width), BF16)] * 3,
        compiler_params=pltpu.CompilerParams(vmem_limit_bytes=16 * 1024 * 1024),
        cost_estimate=pl.CostEstimate(
            flops=16 * returned[0].size * rows,
            bytes_accessed=8 * returned[0].size + 10 * rows * width,
            transcendentals=0,
        ),
        name="mix",
    )(slot, gates, *returned)


def gather_rows(place, held, mine, other):
    depth = mine[0].shape[1]
    block = mine[0].shape[0] // 4
    near = pl.multiple_of(place[0] * depth, 128)
    away = pl.multiple_of((1 - place[0]) * depth, 128)
    for e in range(4):
        for d in range(4):
            at = (e * 4 + d) * block
            held[at : at + block, pl.ds(near, depth)] = mine[e][d * block : (d + 1) * block, :]
            held[at : at + block, pl.ds(away, depth)] = other[d][e * block : (e + 1) * block, :]


def dot_parts(held, parts):
    total, start = 0.0, 0
    for part in parts:
        total = total + dot(held[:, start : start + part.shape[0]], part[...])
        start += part.shape[0]
    return total


def gate_up_kernel(place, *refs):
    mine, other, parts, inv_gain, near_stats, far_stats = (
        refs[:4], refs[4:8], refs[8:12], refs[12], refs[13], refs[14]
    )
    far_outs, own_square, stats, held = refs[15:18], refs[18], refs[19], refs[20]
    rows, depth = held.shape
    wide = own_square.shape[1]
    gather_rows(place, held, mine, other)
    row = lax.broadcasted_iota(jnp.int32, (8, wide), 0)
    picked = jnp.zeros((8, wide), F32)
    for q in range(rows // wide):
        lines = []
        for k in range(wide // 128):
            at = q * wide + k * 128
            sums = jnp.zeros((128, 128), F32)
            for c in range(0, depth, 128):
                value = held[at : at + 128, c : c + 128].astype(F32) * inv_gain[:, c : c + 128]
                sums = sums + value * value
            lines.append(jnp.sum(jnp.transpose(sums), axis=0, keepdims=True))
        line = jnp.broadcast_to(jnp.concatenate(lines, axis=1), (8, wide))
        picked = jnp.where(lax.rem(row, 4) == q, line, picked)
    own_square[...] = picked
    high = picked.astype(BF16)
    low = (picked - high.astype(F32)).astype(BF16)
    both = jnp.where(row < 4, high.astype(F32), low.astype(F32))
    sums = near_stats[...] + far_stats[...]
    stats[...] = sums
    high = sums.astype(BF16).astype(F32)
    pair = jnp.concatenate([high, sums - high], axis=1)
    both = jnp.concatenate([both, pair], axis=0).astype(BF16)
    for d in range(1, NY):
        out = far_outs[d - 1]
        chosen = (parts[:1], parts[1:3], parts[3:])[d - 1]
        out[:rows, :] = dot_parts(held, chosen).astype(BF16)
        out[rows:, :] = both


def gate_up(place, mine, other, parts, inv_gain, near_stats, far_stats):
    rows, depth = 4 * mine[0].shape[0], 2 * mine[0].shape[1]
    wide = parts[0].shape[1]
    vmem = pl.BlockSpec(memory_space=pltpu.VMEM)
    return pl.pallas_call(
        gate_up_kernel,
        in_specs=[pl.BlockSpec(memory_space=pltpu.SMEM)] + [vmem] * 15,
        out_shape=[jax.ShapeDtypeStruct((rows + 32, wide), BF16)] * 3
        + [
            jax.ShapeDtypeStruct((8, wide), F32),
            jax.ShapeDtypeStruct(near_stats.shape, F32),
        ],
        scratch_shapes=[pltpu.VMEM((rows, depth), BF16)],
        compiler_params=pltpu.CompilerParams(vmem_limit_bytes=60 * 1024 * 1024),
        cost_estimate=pl.CostEstimate(
            flops=8 * rows * depth * wide, bytes_accessed=4 * rows * depth, transcendentals=0
        ),
        name="gate_up",
    )(place, *mine, *other, *parts, inv_gain, near_stats, far_stats)


def gate_up_own_kernel(place, *refs):
    mine, other, (gate, up, out, held, weight, sems) = refs[:4], refs[4:8], refs[8:]
    depth = weight.shape[0]
    part = gate.shape[1]
    start = pl.multiple_of(place[2] * depth, 128)
    copies = [
        pltpu.make_async_copy(
            source.at[pl.ds(start, depth), :],
            weight.at[:, k * part : (k + 1) * part],
            sems.at[k],
        )
        for k, source in enumerate((gate, up))
    ]
    for copy in copies:
        copy.start()
    gather_rows(place, held, mine, other)
    for copy in copies:
        copy.wait()
    out[...] = dot(held[...], weight[...])


def gate_up_own(place, mine, other, gate, up):
    rows, depth = 4 * mine[0].shape[0], 2 * mine[0].shape[1]
    wide = 2 * gate.shape[1]
    vmem = pl.BlockSpec(memory_space=pltpu.VMEM)
    hbm = pl.BlockSpec(memory_space=pltpu.HBM)
    return pl.pallas_call(
        gate_up_own_kernel,
        in_specs=[pl.BlockSpec(memory_space=pltpu.SMEM)] + [vmem] * 8 + [hbm] * 2,
        out_shape=jax.ShapeDtypeStruct((rows, wide), F32),
        scratch_shapes=[
            pltpu.VMEM((rows, depth), BF16),
            pltpu.VMEM((depth, wide), BF16),
            pltpu.SemaphoreType.DMA((2,)),
        ],
        compiler_params=pltpu.CompilerParams(vmem_limit_bytes=24 * 1024 * 1024),
        cost_estimate=pl.CostEstimate(
            flops=40 * rows * depth * wide, bytes_accessed=4 * rows * depth, transcendentals=0
        ),
        name="own_part",
    )(place, *mine, *other, gate, up)


def down_kernel(mine, other, own_down, far_down, o0, o1, o2, o3, turned):
    block = o0.shape[0] // 4
    for e in range(4):
        for d in range(4):
            turned[(e * 4 + d) * block : (e * 4 + d + 1) * block, :] = other[
                (d * 4 + e) * block : (d * 4 + e + 1) * block, :
            ]
    for e, out in enumerate((o0, o1, o2, o3)):
        at = slice(e * 4 * block, (e + 1) * 4 * block)
        value = dot(mine[at, :], own_down[...]) + dot(turned[at, :], far_down[...])
        out[...] = value.astype(BF16)


def down(mine, other, own_down, far_down):
    rows, depth = mine.shape
    width = own_down.shape[1]
    return pl.pallas_call(
        down_kernel,
        out_shape=[jax.ShapeDtypeStruct((rows // 4, width), BF16)] * 4,
        scratch_shapes=[pltpu.VMEM((rows, depth), BF16)],
        compiler_params=pltpu.CompilerParams(vmem_limit_bytes=16 * 1024 * 1024),
        cost_estimate=pl.CostEstimate(
            flops=4 * rows * depth * width,
            bytes_accessed=4 * rows * depth + 6 * rows * width,
            transcendentals=0,
        ),
        name="down",
    )(mine, other, own_down, far_down)


def hidden_kernel(full, own, own_square, stats, first, second, third, out, summed):
    rows, wide = own.shape
    far = (first, second, third)
    square = own_square[0:8, :]
    low = jnp.zeros((8, wide), F32)
    total = stats[...]
    for ref in far:
        both = ref[rows : rows + 32, :].astype(F32)
        low = low + both[0:8]
        total = total + both[8:32, :128] + both[8:32, 128:]
    summed[...] = total
    row = lax.broadcasted_iota(jnp.int32, (8, wide), 0)
    square = jnp.where(row < 4, square, 0.0) + low
    square = square[0:4] + square[4:8]
    scale = lax.rsqrt(square / full + EPS)
    part = wide // 2
    for k in range(rows // part):
        line = scale[k // 2 : k // 2 + 1, k % 2 * part : (k % 2 + 1) * part]
        factor = jnp.transpose(jnp.broadcast_to(line, (part, part)))
        at = slice(k * part, (k + 1) * part)
        value = own[at, :]
        for ref in far:
            value = value + ref[at, :].astype(F32)
        gate = value[:, :part] * factor
        up = value[:, part:] * factor
        out[at, :] = (gate / (1.0 + jnp.exp(-gate)) * up).astype(BF16)


def hidden_of(own, own_square, stats, far, full):
    rows, wide = own.shape
    return pl.pallas_call(
        functools.partial(hidden_kernel, full),
        out_shape=[
            jax.ShapeDtypeStruct((rows, wide // 2), BF16),
            jax.ShapeDtypeStruct(stats.shape, F32),
        ],
        compiler_params=pltpu.CompilerParams(vmem_limit_bytes=12 * 1024 * 1024),
        cost_estimate=pl.CostEstimate(
            flops=8 * rows * wide, bytes_accessed=own.size * 10, transcendentals=rows * wide
        ),
        name="hidden",
    )(own, own_square, stats, *far)


def body(
    x_resid,
    query_nope,
    query_rope,
    latent_kv,
    key_rope,
    absorb_key,
    absorb_value,
    out_proj,
    norm_gain,
    router,
    routes,
    gate_proj,
    up_proj,
    down_proj,
):
    rows, width = x_resid.shape
    experts = lax.axis_size("ctx")
    capacity = 2 * rows * TOP // experts
    full = out_proj.shape[1]
    ctx = lax.axis_index("ctx")
    tp = lax.axis_index("tp")
    core = tp % 2
    row_y = tp // 2
    z, x = ctx // NX, ctx % NX

    place = jnp.stack([core, ctx, row_y]).astype(jnp.int32)

    with jax.named_scope("key_gather"):
        expert_ids = jnp.arange(experts, dtype=jnp.int32)
        named = jnp.any(routes[:, :, None] == expert_ids[None, None, :], axis=1).T
        half = (latent_kv.shape[0] + key_rope.shape[0]) // 2
        upper = jnp.concatenate([latent_kv[half:], key_rope], axis=0)
        piece = jnp.where(core == 0, latent_kv[:half], upper)
        piece = jnp.concatenate([piece, named.astype(BF16)], axis=0)
    with jax.named_scope("weights_gate_up"):
        weights = (gate_proj[0], up_proj[0], down_proj[0])
        cuts, _ = cut_weights("cut_first", FIRST_CUTS, 0, place, *weights)
        piece, cuts = lax.optimization_barrier((piece, cuts))
        first = shift(cuts[0], dy=1)
        third = shift(cuts[1], dy=3)

    with jax.named_scope("key_gather"):
        pieces = [piece] + [shift(piece, (d, 0), (0, d)) for d in range(1, 4)]
        line = jnp.concatenate([p[:half] for p in pieces], axis=1)
        masks = jnp.stack([p[half:] for p in pieces])

    with jax.named_scope("weights_gate_up"):
        line, weights = lax.optimization_barrier((line, weights))
        cuts, down_cuts = cut_weights("cut_later", LATER_CUTS, 3, place, *weights)

    with jax.named_scope("key_gather"):
        mine = jnp.concatenate(
            [line] + [shift(line, (0, d), (d, 0)) for d in range(1, 4)], axis=1
        )
        inv_gain = lax.dynamic_slice_in_dim(norm_gain, row_y * 2 * width, 2 * width, 0)
        inv_gain = (1.0 / inv_gain.astype(F32)).reshape(1, 2 * width)
        mine, first, third, cuts, down_cuts, inv_gain = lax.optimization_barrier(
            (mine, first, third, cuts, down_cuts, inv_gain)
        )
        other = shift(mine, dc=1)
        order = jnp.arange(16, dtype=jnp.int32)
        source = (z - order % 4 + 4) % 4 * 4 + (x - order // 4 + 4) % 4
        bias = jnp.where(source <= ctx, 0.0, LOW_SCORE)[None, :, None]
        bias = jnp.where(order[:, None, None] == 0, bias, 0.0)
        bias = jnp.broadcast_to(bias, (16, 16, rows)).reshape(16, 16 * rows).astype(BF16)

    with jax.named_scope("slots"):
        token = jnp.arange(rows, dtype=jnp.int32)
        earlier = (token[:, None] < token[None, :]).astype(BF16)
        slot = jnp.dot(
            masks.reshape(4 * experts, rows), earlier, preferred_element_type=F32
        ).reshape(4, experts, rows)
        slot = jnp.where(masks > 0, slot, -1.0)
        step = jnp.arange(4, dtype=jnp.int32)
        passing = jnp.where(core == 0, z * NX + (x + step) % NX, (z + step) % NZ * NX + x)
        passing = passing[None, :, None, None] == expert_ids[None, None, :, None]

        def pick(values):
            values = jnp.where(passing, values[:, None], 0.0)
            return jnp.sum(values, axis=2).reshape(16, rows)

        slot = pick(slot).astype(jnp.int32)

    with jax.named_scope("weights_gate_up"):
        second0 = shift(cuts[0], dy=2)

    own_part, core_part = attention(
        place, bias, mine, other, query_nope, query_rope, absorb_key, absorb_value, out_proj
    )

    own_part, core_part, second0 = lax.optimization_barrier((own_part, core_part, second0))

    with jax.named_scope("attn_sum"):
        pair = own_part + shift(core_part, dc=1).astype(F32)
        pair_low = pair.astype(BF16)
        resid = x_resid.astype(F32) + pair[0]
        for d in range(1, NY):
            resid = resid + shift(pair_low[d], dy=d).astype(F32)

    with jax.named_scope("dispatch"):
        col_start = tp * width
        gain = lax.dynamic_slice_in_dim(norm_gain, col_start, width, 0).astype(F32)
        scaled = resid * gain[None, :]
        outgoing = scaled.astype(BF16)
        router_cols = lax.dynamic_slice_in_dim(router, col_start, width, 1).astype(F32)
        outgoing, late_down, late = lax.optimization_barrier((outgoing, down_cuts, cuts[1]))
        tokens = [outgoing] + [shift(outgoing, (d, 0), (0, d)) for d in range(1, 4)]

    with jax.named_scope("weights_down"):
        moved = [shift(late_down[0], dy=1), None, shift(late_down[2], dy=3)]
        tokens, moved, late, far_cut = lax.optimization_barrier(
            (tokens, moved, late, late_down[1])
        )
        moved[1] = shift(far_cut, dy=2)
        second1 = shift(late, dy=2)

    with jax.named_scope("gates"):
        scaled, resid_late = lax.optimization_barrier((scaled, resid))
        logits = lax.dot_general(
            router_cols, scaled, (((1,), (1,)), ((), ())), precision=lax.Precision.HIGHEST
        )
        squares = jnp.sum(resid_late * resid_late, axis=1)[None, :]
        stats = jnp.concatenate([logits, jnp.broadcast_to(squares, (8, rows))], axis=0)
        far_stats = shift(stats, dc=1)

    with jax.named_scope("dispatch"):
        filled = fill(slot, tokens, capacity)
        arrived = [filled[0]] + [shift(filled[e], (0, e), (e, 0)) for e in range(1, 4)]
        arrived, moved[1], second1, far_stats = lax.optimization_barrier(
            (arrived, moved[1], second1, far_stats)
        )
        far_cols = [shift(block, dc=1) for block in arrived]

    with jax.named_scope("experts"):
        parts = (first, second0, second1, third)
        *far, own_square, stats = gate_up(
            place, arrived, far_cols, parts, inv_gain, stats, far_stats
        )
        moved, arrived, own_square = lax.optimization_barrier((moved, arrived, own_square))
        far = [shift(far[d - 1], dy=-d) for d in range(1, NY)]
        own = gate_up_own(place, arrived, far_cols, gate_proj[0], up_proj[0])

    with jax.named_scope("weights_down"):
        own_down, far_down = unpack(place, moved, down_proj[0])
        far_down = shift(far_down, dc=1)
        own, own_down, far_down = lax.optimization_barrier((own, own_down, far_down))

    with jax.named_scope("experts"):
        hidden, summed = hidden_of(own, own_square, stats, far, float(full))
        hidden = jnp.concatenate(
            [hidden] + [shift(hidden, dy=d) for d in range(1, NY)], axis=1
        )

    with jax.named_scope("gates"):
        inv_rms = lax.rsqrt(summed[experts] / full + EPS)
        gates = jnp.where(named, jax.nn.sigmoid(summed[:experts] * inv_rms[None, :]), 0.0)
        gates = ROUTE_SCALE * gates / jnp.sum(gates, axis=0, keepdims=True)
        gates = [gates] + [shift(gates, (d, 0), (0, d)) for d in range(1, 4)]
        hidden, gates = lax.optimization_barrier((hidden, gates))
        gates = pick(jnp.stack(gates))

    with jax.named_scope("experts"):
        far_hidden = shift(hidden, dc=1)
        result = down(hidden, far_hidden, own_down, far_down)

    with jax.named_scope("combine"):
        result = [result[0]] + [shift(result[e], (0, -e), (-e, 0)) for e in range(1, 4)]
        own_sum, *far_sum = mix(slot, gates, result)
        total = resid + own_sum
        for d in range(1, 4):
            total = total + shift(far_sum[d - 1], (-d, 0), (0, -d)).astype(F32)
        return total.astype(BF16)


def solution(mesh):
    return jax.shard_map(
        body,
        mesh=mesh,
        in_specs=(
            P("ctx", "tp"),
            P("ctx", "tp"),
            P("ctx", "tp"),
            P(None, "ctx"),
            P(None, "ctx"),
            P("tp", None, None),
            P("tp", None, None),
            P("tp", None),
            P(),
            P(),
            P("ctx", None),
            P("ctx", None, "tp"),
            P("ctx", None, "tp"),
            P("ctx", "tp", None),
        ),
        out_specs=P("ctx", "tp"),
        check_vma=False,
    )
```

```python
import functools

import jax
import jax.numpy as jnp
from jax import lax
from jax.experimental import pallas as pl
from jax.experimental.pallas import tpu as pltpu
from jax.sharding import PartitionSpec as P

NOPE = 128
ROPE = 64
VDIM = 128
TOP = 4
NZ = 4
NX = 4
NY = 4

EPS = 1e-06
ROUTE_SCALE = 2.5
LOW_SCORE = -1e30
LOG2E = 1.4426950408889634
F32 = jnp.float32
BF16 = jnp.bfloat16
AXES = ("ctx", "tp")


def shift(value, first=(0, 0), second=None, dy=0, dc=0):
    second = first if second is None else second
    pairs = []
    for z in range(NZ):
        for x in range(NX):
            for y in range(NY):
                for c in range(2):
                    dz, dx = second if c else first
                    to_ctx = (z + dz) % NZ * NX + (x + dx) % NX
                    to_tp = (y + dy) % NY * 2 + (c ^ dc)
                    pairs.append(((z * NX + x) * 8 + y * 2 + c, to_ctx * 8 + to_tp))
    return lax.ppermute(value, AXES, pairs)


def dot(a, b, ca=1, cb=0):
    return lax.dot_general(a, b, (((ca,), (cb,)), ((), ())), preferred_element_type=F32)


def attention_kernel(
    place, bias, mine, other, q_nope, q_rope, absorb_key, absorb_value, out_proj,
    own_out, core_out, keys, total, weight, sems,
):
    step = pl.program_id(0)
    deep = weight.shape[1]
    loads = [
        pltpu.make_async_copy(
            out_proj.at[k * deep : (k + 1) * deep, :], weight.at[k], sems.at[k]
        )
        for k in range(weight.shape[0])
    ]

    @pl.when(step == 0)
    def _():
        for load in loads:
            load.start()

    core, row_y = place[0], place[2]
    rows = q_nope.shape[0]
    half = mine.shape[0]
    block = mine.shape[1] // 16

    def put(row0, ref, turned):
        for i in range(16):
            j = i % 4 * 4 + i // 4 if turned else i
            keys[row0 : row0 + half, i * block : (i + 1) * block] = ref[
                :, j * block : (j + 1) * block
            ]

    @pl.when(step == 0)
    def _():
        keys[2 * half :, :] = bias[...]

    @pl.when((step == 0) & (core == 0))
    def _():
        put(0, mine, False)
        put(half, other, True)

    @pl.when((step == 0) & (core == 1))
    def _():
        put(0, other, False)
        put(half, mine, True)

    heads = absorb_key.shape[0]
    latent_size = absorb_key.shape[2]
    queries = []
    for h in range(heads):
        lat = dot(q_nope[:, h * NOPE : (h + 1) * NOPE], absorb_key[h]).astype(BF16)
        rope = q_rope[:, h * ROPE : (h + 1) * ROPE]
        queries.append(jnp.concatenate([lat, rope, jnp.ones((rows, 16), BF16)], axis=1))
    queries = jnp.concatenate(queries, axis=0)
    scores = dot(queries, keys[...])
    shape = (heads * rows, block)
    query = lax.rem(lax.broadcasted_iota(jnp.int32, shape, 0), rows)
    allowed = lax.broadcasted_iota(jnp.int32, shape, 1) <= query
    own = jnp.where(allowed, scores[:, :block], LOW_SCORE)
    scores = jnp.concatenate([own, scores[:, block:]], axis=1)
    top = jnp.max(scores, axis=1, keepdims=True)
    factor = LOG2E * (NOPE + ROPE) ** (-0.5)
    weights = jnp.exp2((scores - top) * factor)
    norm = jnp.sum(weights, axis=1, keepdims=True)
    lat_out = dot(weights.astype(BF16), keys[:latent_size, :], 1, 1)
    lat_out = (lat_out / norm).astype(BF16)
    outs = [
        dot(lat_out[h * rows : (h + 1) * rows], absorb_value[h]).astype(BF16)
        for h in range(heads)
    ]
    for k, load in enumerate(loads):

        @pl.when(step == k)
        def _():
            load.wait()

    part = dot(jnp.concatenate(outs, axis=1), weight[step])

    @pl.when(step == 0)
    def _():
        total[...] = part

    @pl.when(step > 0)
    def _():
        total[...] += part

    @pl.when(step == pl.num_programs(0) - 1)
    def _():
        width = own_out.shape[2]
        for d in range(NY):
            chunk = lax.rem(row_y + d, NY) * 2
            own = pl.multiple_of((chunk + core) * width, 128)
            far = pl.multiple_of((chunk + 1 - core) * width, 128)
            own_out[d] = total[:, pl.ds(own, width)]
            core_out[d] = total[:, pl.ds(far, width)].astype(BF16)


def attention(place, bias, mine, other, q_nope, q_rope, absorb_key, absorb_value, out_proj):
    rows = q_nope.shape[0]
    head_count = absorb_key.shape[0]
    latent_size = absorb_key.shape[2]
    width = out_proj.shape[1]
    per = 4
    key_count = bias.shape[1]
    depth = 2 * mine.shape[0] + bias.shape[0]
    fixed = lambda shape: pl.BlockSpec(shape, lambda i: (0,) * len(shape))
    chunk = (NY, rows, width // (2 * NY))
    return pl.pallas_call(
        attention_kernel,
        grid=(head_count // per,),
        in_specs=[
            pl.BlockSpec(memory_space=pltpu.SMEM),
            fixed(bias.shape),
            fixed(mine.shape),
            fixed(other.shape),
            pl.BlockSpec((rows, per * NOPE), lambda i: (0, i)),
            pl.BlockSpec((rows, per * ROPE), lambda i: (0, i)),
            pl.BlockSpec((per,) + absorb_key.shape[1:], lambda i: (i, 0, 0)),
            pl.BlockSpec((per,) + absorb_value.shape[1:], lambda i: (i, 0, 0)),
            pl.BlockSpec(memory_space=pltpu.HBM),
        ],
        out_specs=[fixed(chunk), fixed(chunk)],
        out_shape=[
            jax.ShapeDtypeStruct(chunk, F32),
            jax.ShapeDtypeStruct(chunk, BF16),
        ],
        scratch_shapes=[
            pltpu.VMEM((depth, key_count), BF16),
            pltpu.VMEM((rows, width), F32),
            pltpu.VMEM((head_count // per, per * VDIM, width), BF16),
            pltpu.SemaphoreType.DMA((head_count // per,)),
        ],
        compiler_params=pltpu.CompilerParams(vmem_limit_bytes=60 * 1024 * 1024),
        cost_estimate=pl.CostEstimate(
            flops=2 * rows * head_count * key_count * (depth + latent_size)
            + 2 * rows * head_count * VDIM * width,
            bytes_accessed=out_proj.size * 2 + 4 * mine.size,
            transcendentals=rows * head_count * key_count,
        ),
        name="attention",
    )(place, bias, mine, other, q_nope, q_rope, absorb_key, absorb_value, out_proj)


FIRST_CUTS = ((1, 0, 1792), (3, 0, 1792))
LATER_CUTS = ((2, 0, 1152), (2, 1152, 1792))


def cut_kernel(cuts, place, gate, up, down, *rest):
    outs, sems = rest[:-1], rest[-1]
    part = gate.shape[1]
    depth = gate.shape[0] // NY
    copies = []
    for out, (d, first, _) in zip(outs, cuts):
        start = pl.multiple_of(lax.rem(place[2] + d, NY) * depth + first, 64)
        for k, source in enumerate((gate, up)):
            copies.append(
                (source.at[pl.ds(start, out.shape[0]), :], out.at[:, k * part : (k + 1) * part])
            )
    for d, out in enumerate(outs[len(cuts) :]):
        start = pl.multiple_of(lax.rem(place[2] + d + 1, NY) * depth, 128)
        copies.append((down.at[:, pl.ds(start, depth)], out))
    copies = [pltpu.make_async_copy(a, b, sems.at[i]) for i, (a, b) in enumerate(copies)]
    for copy in copies:
        copy.start()
    for copy in copies:
        copy.wait()


def cut_weights(name, cuts, down_count, place, gate, up, down):
    hbm = pl.BlockSpec(memory_space=pltpu.HBM)
    outs = pl.pallas_call(
        functools.partial(cut_kernel, cuts),
        in_specs=[pl.BlockSpec(memory_space=pltpu.SMEM), hbm, hbm, hbm],
        out_shape=[
            jax.ShapeDtypeStruct((end - first, 2 * gate.shape[1]), BF16) for _, first, end in cuts
        ]
        + [jax.ShapeDtypeStruct((down.shape[0], down.shape[1] // NY), BF16)] * down_count,
        scratch_shapes=[pltpu.SemaphoreType.DMA((2 * len(cuts) + down_count,))],
        compiler_params=pltpu.CompilerParams(vmem_limit_bytes=60 * 1024 * 1024),
        cost_estimate=pl.CostEstimate(
            flops=0, bytes_accessed=4 * gate.size, transcendentals=0
        ),
        name=name,
    )(place, gate, up, down)
    return outs[: len(cuts)], outs[len(cuts) :]


def unpack_kernel(place, first, second, third, down, own, far, kept, sem):
    rows, depth = kept.shape
    width = depth // 2
    start = pl.multiple_of(place[2] * depth, 128)
    copy = pltpu.make_async_copy(down.at[:, pl.ds(start, depth)], kept, sem)
    copy.start()
    near = pl.multiple_of(place[0] * width, 128)
    away = pl.multiple_of((1 - place[0]) * width, 128)
    for d, ref in ((1, first), (2, second), (3, third), (0, kept)):
        if d == 0:
            copy.wait()
        own[d * rows : (d + 1) * rows, :] = ref[:, pl.ds(near, width)]
        far[d * rows : (d + 1) * rows, :] = ref[:, pl.ds(away, width)]


def unpack(place, moved, down):
    rows, depth = moved[0].shape
    vmem = pl.BlockSpec(memory_space=pltpu.VMEM)
    return pl.pallas_call(
        unpack_kernel,
        in_specs=[pl.BlockSpec(memory_space=pltpu.SMEM), vmem, vmem, vmem]
        + [pl.BlockSpec(memory_space=pltpu.HBM)],
        out_shape=[jax.ShapeDtypeStruct((NY * rows, depth // 2), BF16)] * 2,
        scratch_shapes=[pltpu.VMEM((rows, depth), BF16), pltpu.SemaphoreType.DMA],
        compiler_params=pltpu.CompilerParams(vmem_limit_bytes=12 * 1024 * 1024),
        cost_estimate=pl.CostEstimate(
            flops=0, bytes_accessed=16 * rows * depth, transcendentals=0
        ),
        name="unpack",
    )(place, *moved, down)


def slots_of(line, capacity):
    ids = lax.broadcasted_iota(jnp.int32, (capacity, line.shape[1]), 0)
    return jnp.broadcast_to(line, ids.shape) == ids


def fill_kernel(slot, t0, t1, t2, t3, *outs):
    for e, out in enumerate(outs):
        capacity = out.shape[0] // NY
        for d, ref in enumerate((t0, t1, t2, t3)):
            at = d * 4 + e
            placed = slots_of(slot[at : at + 1, :], capacity).astype(BF16)
            out[d * capacity : (d + 1) * capacity, :] = dot(placed, ref[...]).astype(BF16)


def fill(slot, tokens, capacity):
    rows, width = tokens[0].shape
    return pl.pallas_call(
        fill_kernel,
        out_shape=[jax.ShapeDtypeStruct((4 * capacity, width), BF16)] * 4,
        compiler_params=pltpu.CompilerParams(vmem_limit_bytes=16 * 1024 * 1024),
        cost_estimate=pl.CostEstimate(
            flops=32 * capacity * rows * width,
            bytes_accessed=8 * rows * width + 32 * capacity * width,
            transcendentals=0,
        ),
        name="fill",
    )(slot, *tokens)


def mix_kernel(slot, gates, r0, r1, r2, r3, own, *far):
    capacity = r0.shape[0] // 4
    for d in range(4):
        high, low, rows = [], [], []
        for e, ref in enumerate((r0, r1, r2, r3)):
            at = d * 4 + e
            placed = slots_of(slot[at : at + 1, :], capacity)
            value = jnp.where(placed, jnp.broadcast_to(gates[at : at + 1, :], placed.shape), 0.0)
            first = value.astype(BF16)
            high.append(first)
            low.append((value - first.astype(F32)).astype(BF16))
            rows.append(ref[d * capacity : (d + 1) * capacity, :])
        rows = jnp.concatenate(rows, axis=0)
        total = dot(jnp.concatenate(high, axis=0), rows, 0, 0)
        total = total + dot(jnp.concatenate(low, axis=0), rows, 0, 0)
        if d == 0:
            own[...] = total
        else:
            far[d - 1][...] = total.astype(BF16)


def mix(slot, gates, returned):
    width = returned[0].shape[1]
    rows = slot.shape[1]
    return pl.pallas_call(
        mix_kernel,
        out_shape=[jax.ShapeDtypeStruct((rows, width), F32)]
        + [jax.ShapeDtypeStruct((rows, width), BF16)] * 3,
        compiler_params=pltpu.CompilerParams(vmem_limit_bytes=16 * 1024 * 1024),
        cost_estimate=pl.CostEstimate(
            flops=16 * returned[0].size * rows,
            bytes_accessed=8 * returned[0].size + 10 * rows * width,
            transcendentals=0,
        ),
        name="mix",
    )(slot, gates, *returned)


def gather_rows(place, held, mine, other):
    depth = mine[0].shape[1]
    block = mine[0].shape[0] // 4
    near = pl.multiple_of(place[0] * depth, 128)
    away = pl.multiple_of((1 - place[0]) * depth, 128)
    for e in range(4):
        for d in range(4):
            at = (e * 4 + d) * block
            held[at : at + block, pl.ds(near, depth)] = mine[e][d * block : (d + 1) * block, :]
            held[at : at + block, pl.ds(away, depth)] = other[d][e * block : (e + 1) * block, :]


def dot_parts(held, parts):
    total, start = 0.0, 0
    for part in parts:
        total = total + dot(held[:, start : start + part.shape[0]], part[...])
        start += part.shape[0]
    return total


def gate_up_kernel(place, *refs):
    mine, other, parts, inv_gain, near_stats, far_stats = (
        refs[:4], refs[4:8], refs[8:12], refs[12], refs[13], refs[14]
    )
    far_outs, own_square, stats, held = refs[15:18], refs[18], refs[19], refs[20]
    rows, depth = held.shape
    wide = own_square.shape[1]
    gather_rows(place, held, mine, other)
    row = lax.broadcasted_iota(jnp.int32, (8, wide), 0)
    picked = jnp.zeros((8, wide), F32)
    for q in range(rows // wide):
        lines = []
        for k in range(wide // 128):
            at = q * wide + k * 128
            sums = jnp.zeros((128, 128), F32)
            for c in range(0, depth, 128):
                value = held[at : at + 128, c : c + 128].astype(F32) * inv_gain[:, c : c + 128]
                sums = sums + value * value
            lines.append(jnp.sum(jnp.transpose(sums), axis=0, keepdims=True))
        line = jnp.broadcast_to(jnp.concatenate(lines, axis=1), (8, wide))
        picked = jnp.where(lax.rem(row, 4) == q, line, picked)
    own_square[...] = picked
    high = picked.astype(BF16)
    low = (picked - high.astype(F32)).astype(BF16)
    both = jnp.where(row < 4, high.astype(F32), low.astype(F32))
    sums = near_stats[...] + far_stats[...]
    stats[...] = sums
    high = sums.astype(BF16).astype(F32)
    pair = jnp.concatenate([high, sums - high], axis=1)
    both = jnp.concatenate([both, pair], axis=0).astype(BF16)
    for d in range(1, NY):
        out = far_outs[d - 1]
        chosen = (parts[:1], parts[1:3], parts[3:])[d - 1]
        out[:rows, :] = dot_parts(held, chosen).astype(BF16)
        out[rows:, :] = both


def gate_up(place, mine, other, parts, inv_gain, near_stats, far_stats):
    rows, depth = 4 * mine[0].shape[0], 2 * mine[0].shape[1]
    wide = parts[0].shape[1]
    vmem = pl.BlockSpec(memory_space=pltpu.VMEM)
    return pl.pallas_call(
        gate_up_kernel,
        in_specs=[pl.BlockSpec(memory_space=pltpu.SMEM)] + [vmem] * 15,
        out_shape=[jax.ShapeDtypeStruct((rows + 32, wide), BF16)] * 3
        + [
            jax.ShapeDtypeStruct((8, wide), F32),
            jax.ShapeDtypeStruct(near_stats.shape, F32),
        ],
        scratch_shapes=[pltpu.VMEM((rows, depth), BF16)],
        compiler_params=pltpu.CompilerParams(vmem_limit_bytes=60 * 1024 * 1024),
        cost_estimate=pl.CostEstimate(
            flops=8 * rows * depth * wide, bytes_accessed=4 * rows * depth, transcendentals=0
        ),
        name="gate_up",
    )(place, *mine, *other, *parts, inv_gain, near_stats, far_stats)


def gate_up_own_kernel(place, *refs):
    mine, other, (gate, up, out, held, weight, sems) = refs[:4], refs[4:8], refs[8:]
    depth = weight.shape[0]
    part = gate.shape[1]
    start = pl.multiple_of(place[2] * depth, 128)
    copies = [
        pltpu.make_async_copy(
            source.at[pl.ds(start, depth), :],
            weight.at[:, k * part : (k + 1) * part],
            sems.at[k],
        )
        for k, source in enumerate((gate, up))
    ]
    for copy in copies:
        copy.start()
    gather_rows(place, held, mine, other)
    for copy in copies:
        copy.wait()
    out[...] = dot(held[...], weight[...])


def gate_up_own(place, mine, other, gate, up):
    rows, depth = 4 * mine[0].shape[0], 2 * mine[0].shape[1]
    wide = 2 * gate.shape[1]
    vmem = pl.BlockSpec(memory_space=pltpu.VMEM)
    hbm = pl.BlockSpec(memory_space=pltpu.HBM)
    return pl.pallas_call(
        gate_up_own_kernel,
        in_specs=[pl.BlockSpec(memory_space=pltpu.SMEM)] + [vmem] * 8 + [hbm] * 2,
        out_shape=jax.ShapeDtypeStruct((rows, wide), F32),
        scratch_shapes=[
            pltpu.VMEM((rows, depth), BF16),
            pltpu.VMEM((depth, wide), BF16),
            pltpu.SemaphoreType.DMA((2,)),
        ],
        compiler_params=pltpu.CompilerParams(vmem_limit_bytes=24 * 1024 * 1024),
        cost_estimate=pl.CostEstimate(
            flops=40 * rows * depth * wide, bytes_accessed=4 * rows * depth, transcendentals=0
        ),
        name="own_part",
    )(place, *mine, *other, gate, up)


def down_kernel(mine, other, own_down, far_down, o0, o1, o2, o3, turned):
    block = o0.shape[0] // 4
    for e in range(4):
        for d in range(4):
            turned[(e * 4 + d) * block : (e * 4 + d + 1) * block, :] = other[
                (d * 4 + e) * block : (d * 4 + e + 1) * block, :
            ]
    for e, out in enumerate((o0, o1, o2, o3)):
        at = slice(e * 4 * block, (e + 1) * 4 * block)
        value = dot(mine[at, :], own_down[...]) + dot(turned[at, :], far_down[...])
        out[...] = value.astype(BF16)


def down(mine, other, own_down, far_down):
    rows, depth = mine.shape
    width = own_down.shape[1]
    return pl.pallas_call(
        down_kernel,
        out_shape=[jax.ShapeDtypeStruct((rows // 4, width), BF16)] * 4,
        scratch_shapes=[pltpu.VMEM((rows, depth), BF16)],
        compiler_params=pltpu.CompilerParams(vmem_limit_bytes=16 * 1024 * 1024),
        cost_estimate=pl.CostEstimate(
            flops=4 * rows * depth * width,
            bytes_accessed=4 * rows * depth + 6 * rows * width,
            transcendentals=0,
        ),
        name="down",
    )(mine, other, own_down, far_down)


def hidden_kernel(full, own, own_square, stats, first, second, third, out, summed):
    rows, wide = own.shape
    far = (first, second, third)
    square = own_square[0:8, :]
    low = jnp.zeros((8, wide), F32)
    total = stats[...]
    for ref in far:
        both = ref[rows : rows + 32, :].astype(F32)
        low = low + both[0:8]
        total = total + both[8:32, :128] + both[8:32, 128:]
    summed[...] = total
    row = lax.broadcasted_iota(jnp.int32, (8, wide), 0)
    square = jnp.where(row < 4, square, 0.0) + low
    square = square[0:4] + square[4:8]
    scale = lax.rsqrt(square / full + EPS)
    part = wide // 2
    for k in range(rows // part):
        line = scale[k // 2 : k // 2 + 1, k % 2 * part : (k % 2 + 1) * part]
        factor = jnp.transpose(jnp.broadcast_to(line, (part, part)))
        at = slice(k * part, (k + 1) * part)
        value = own[at, :]
        for ref in far:
            value = value + ref[at, :].astype(F32)
        gate = value[:, :part] * factor
        up = value[:, part:] * factor
        out[at, :] = (gate / (1.0 + jnp.exp(-gate)) * up).astype(BF16)


def hidden_of(own, own_square, stats, far, full):
    rows, wide = own.shape
    return pl.pallas_call(
        functools.partial(hidden_kernel, full),
        out_shape=[
            jax.ShapeDtypeStruct((rows, wide // 2), BF16),
            jax.ShapeDtypeStruct(stats.shape, F32),
        ],
        compiler_params=pltpu.CompilerParams(vmem_limit_bytes=12 * 1024 * 1024),
        cost_estimate=pl.CostEstimate(
            flops=8 * rows * wide, bytes_accessed=own.size * 10, transcendentals=rows * wide
        ),
        name="hidden",
    )(own, own_square, stats, *far)


def body(
    x_resid,
    query_nope,
    query_rope,
    latent_kv,
    key_rope,
    absorb_key,
    absorb_value,
    out_proj,
    norm_gain,
    router,
    routes,
    gate_proj,
    up_proj,
    down_proj,
):
    rows, width = x_resid.shape
    experts = lax.axis_size("ctx")
    capacity = 2 * rows * TOP // experts
    full = out_proj.shape[1]
    ctx = lax.axis_index("ctx")
    tp = lax.axis_index("tp")
    core = tp % 2
    row_y = tp // 2
    z, x = ctx // NX, ctx % NX

    place = jnp.stack([core, ctx, row_y]).astype(jnp.int32)

    with jax.named_scope("key_gather"):
        expert_ids = jnp.arange(experts, dtype=jnp.int32)
        named = jnp.any(routes[:, :, None] == expert_ids[None, None, :], axis=1).T
        half = (latent_kv.shape[0] + key_rope.shape[0]) // 2
        upper = jnp.concatenate([latent_kv[half:], key_rope], axis=0)
        piece = jnp.where(core == 0, latent_kv[:half], upper)
        piece = jnp.concatenate([piece, named.astype(BF16)], axis=0)
    with jax.named_scope("weights_gate_up"):
        weights = (gate_proj[0], up_proj[0], down_proj[0])
        cuts, _ = cut_weights("cut_first", FIRST_CUTS, 0, place, *weights)
        piece, cuts = lax.optimization_barrier((piece, cuts))
        first = shift(cuts[0], dy=1)
        third = shift(cuts[1], dy=3)

    with jax.named_scope("key_gather"):
        pieces = [piece] + [shift(piece, (d, 0), (0, d)) for d in range(1, 4)]
        line = jnp.concatenate([p[:half] for p in pieces], axis=1)
        masks = jnp.stack([p[half:] for p in pieces])

    with jax.named_scope("weights_gate_up"):
        line, weights = lax.optimization_barrier((line, weights))
        cuts, down_cuts = cut_weights("cut_later", LATER_CUTS, 3, place, *weights)

    with jax.named_scope("key_gather"):
        mine = jnp.concatenate(
            [line] + [shift(line, (0, d), (d, 0)) for d in range(1, 4)], axis=1
        )
        inv_gain = lax.dynamic_slice_in_dim(norm_gain, row_y * 2 * width, 2 * width, 0)
        inv_gain = (1.0 / inv_gain.astype(F32)).reshape(1, 2 * width)
        mine, first, third, cuts, down_cuts, inv_gain = lax.optimization_barrier(
            (mine, first, third, cuts, down_cuts, inv_gain)
        )
        other = shift(mine, dc=1)
        order = jnp.arange(16, dtype=jnp.int32)
        source = (z - order % 4 + 4) % 4 * 4 + (x - order // 4 + 4) % 4
        bias = jnp.where(source <= ctx, 0.0, LOW_SCORE)[None, :, None]
        bias = jnp.where(order[:, None, None] == 0, bias, 0.0)
        bias = jnp.broadcast_to(bias, (16, 16, rows)).reshape(16, 16 * rows).astype(BF16)

    with jax.named_scope("slots"):
        token = jnp.arange(rows, dtype=jnp.int32)
        earlier = (token[:, None] < token[None, :]).astype(BF16)
        slot = jnp.dot(
            masks.reshape(4 * experts, rows), earlier, preferred_element_type=F32
        ).reshape(4, experts, rows)
        slot = jnp.where(masks > 0, slot, -1.0)
        step = jnp.arange(4, dtype=jnp.int32)
        passing = jnp.where(core == 0, z * NX + (x + step) % NX, (z + step) % NZ * NX + x)
        passing = passing[None, :, None, None] == expert_ids[None, None, :, None]

        def pick(values):
            values = jnp.where(passing, values[:, None], 0.0)
            return jnp.sum(values, axis=2).reshape(16, rows)

        slot = pick(slot).astype(jnp.int32)

    with jax.named_scope("weights_gate_up"):
        second0 = shift(cuts[0], dy=2)

    own_part, core_part = attention(
        place, bias, mine, other, query_nope, query_rope, absorb_key, absorb_value, out_proj
    )

    own_part, core_part, second0 = lax.optimization_barrier((own_part, core_part, second0))

    with jax.named_scope("attn_sum"):
        pair = own_part + shift(core_part, dc=1).astype(F32)
        pair_low = pair.astype(BF16)
        resid = x_resid.astype(F32) + pair[0]
        for d in range(1, NY):
            resid = resid + shift(pair_low[d], dy=d).astype(F32)

    with jax.named_scope("dispatch"):
        col_start = tp * width
        gain = lax.dynamic_slice_in_dim(norm_gain, col_start, width, 0).astype(F32)
        scaled = resid * gain[None, :]
        outgoing = scaled.astype(BF16)
        router_cols = lax.dynamic_slice_in_dim(router, col_start, width, 1).astype(F32)
        outgoing, late_down, late = lax.optimization_barrier((outgoing, down_cuts, cuts[1]))
        tokens = [outgoing] + [shift(outgoing, (d, 0), (0, d)) for d in range(1, 4)]

    with jax.named_scope("weights_down"):
        moved = [shift(late_down[0], dy=1), None, shift(late_down[2], dy=3)]
        tokens, moved, late, far_cut = lax.optimization_barrier(
            (tokens, moved, late, late_down[1])
        )
        moved[1] = shift(far_cut, dy=2)
        second1 = shift(late, dy=2)

    with jax.named_scope("gates"):
        scaled, resid_late = lax.optimization_barrier((scaled, resid))
        logits = lax.dot_general(
            router_cols, scaled, (((1,), (1,)), ((), ())), precision=lax.Precision.HIGHEST
        )
        squares = jnp.sum(resid_late * resid_late, axis=1)[None, :]
        stats = jnp.concatenate([logits, jnp.broadcast_to(squares, (8, rows))], axis=0)
        far_stats = shift(stats, dc=1)

    with jax.named_scope("dispatch"):
        filled = fill(slot, tokens, capacity)
        arrived = [filled[0]] + [shift(filled[e], (0, e), (e, 0)) for e in range(1, 4)]
        arrived, moved[1], second1, far_stats = lax.optimization_barrier(
            (arrived, moved[1], second1, far_stats)
        )
        far_cols = [shift(block, dc=1) for block in arrived]

    with jax.named_scope("experts"):
        parts = (first, second0, second1, third)
        *far, own_square, stats = gate_up(
            place, arrived, far_cols, parts, inv_gain, stats, far_stats
        )
        moved, arrived, own_square = lax.optimization_barrier((moved, arrived, own_square))
        far = [shift(far[d - 1], dy=-d) for d in range(1, NY)]
        own = gate_up_own(place, arrived, far_cols, gate_proj[0], up_proj[0])

    with jax.named_scope("weights_down"):
        own_down, far_down = unpack(place, moved, down_proj[0])
        far_down = shift(far_down, dc=1)
        own, own_down, far_down = lax.optimization_barrier((own, own_down, far_down))

    with jax.named_scope("experts"):
        hidden, summed = hidden_of(own, own_square, stats, far, float(full))
        hidden = jnp.concatenate(
            [hidden] + [shift(hidden, dy=d) for d in range(1, NY)], axis=1
        )

    with jax.named_scope("gates"):
        inv_rms = lax.rsqrt(summed[experts] / full + EPS)
        gates = jnp.where(named, jax.nn.sigmoid(summed[:experts] * inv_rms[None, :]), 0.0)
        gates = ROUTE_SCALE * gates / jnp.sum(gates, axis=0, keepdims=True)
        gates = [gates] + [shift(gates, (d, 0), (0, d)) for d in range(1, 4)]
        hidden, gates = lax.optimization_barrier((hidden, gates))
        gates = pick(jnp.stack(gates))

    with jax.named_scope("experts"):
        far_hidden = shift(hidden, dc=1)
        result = down(hidden, far_hidden, own_down, far_down)

    with jax.named_scope("combine"):
        result = [result[0]] + [shift(result[e], (0, -e), (-e, 0)) for e in range(1, 4)]
        own_sum, *far_sum = mix(slot, gates, result)
        total = resid + own_sum
        for d in range(1, 4):
            total = total + shift(far_sum[d - 1], (-d, 0), (0, -d)).astype(F32)
        return total.astype(BF16)


def solution(mesh):
    return jax.shard_map(
        body,
        mesh=mesh,
        in_specs=(
            P("ctx", "tp"),
            P("ctx", "tp"),
            P("ctx", "tp"),
            P(None, "ctx"),
            P(None, "ctx"),
            P("tp", None, None),
            P("tp", None, None),
            P("tp", None),
            P(),
            P(),
            P("ctx", None),
            P("ctx", None, "tp"),
            P("ctx", None, "tp"),
            P("ctx", "tp", None),
        ),
        out_specs=P("ctx", "tp"),
        check_vma=False,
    )
```

```python
import functools

import jax
import jax.numpy as jnp
from jax import lax
from jax.experimental import pallas as pl
from jax.experimental.pallas import tpu as pltpu
from jax.sharding import PartitionSpec as P

NOPE = 128
ROPE = 64
VDIM = 128
TOP = 4
NZ = 4
NX = 4
NY = 4

EPS = 1e-06
ROUTE_SCALE = 2.5
LOW_SCORE = -1e30
LOG2E = 1.4426950408889634
F32 = jnp.float32
BF16 = jnp.bfloat16
AXES = ("ctx", "tp")


def shift(value, first=(0, 0), second=None, dy=0, dc=0):
    second = first if second is None else second
    pairs = []
    for z in range(NZ):
        for x in range(NX):
            for y in range(NY):
                for c in range(2):
                    dz, dx = second if c else first
                    to_ctx = (z + dz) % NZ * NX + (x + dx) % NX
                    to_tp = (y + dy) % NY * 2 + (c ^ dc)
                    pairs.append(((z * NX + x) * 8 + y * 2 + c, to_ctx * 8 + to_tp))
    return lax.ppermute(value, AXES, pairs)


def dot(a, b, ca=1, cb=0):
    return lax.dot_general(a, b, (((ca,), (cb,)), ((), ())), preferred_element_type=F32)


def attention_kernel(
    place, bias, mine, other, q_nope, q_rope, absorb_key, absorb_value, out_proj,
    own_out, core_out, keys, total, weight, sems,
):
    step = pl.program_id(0)
    deep = weight.shape[1]
    loads = [
        pltpu.make_async_copy(
            out_proj.at[k * deep : (k + 1) * deep, :], weight.at[k], sems.at[k]
        )
        for k in range(weight.shape[0])
    ]

    @pl.when(step == 0)
    def _():
        for load in loads:
            load.start()

    core, row_y = place[0], place[2]
    rows = q_nope.shape[0]
    half = mine.shape[0]
    block = mine.shape[1] // 16

    def put(row0, ref, turned):
        for i in range(16):
            j = i % 4 * 4 + i // 4 if turned else i
            keys[row0 : row0 + half, i * block : (i + 1) * block] = ref[
                :, j * block : (j + 1) * block
            ]

    @pl.when(step == 0)
    def _():
        keys[2 * half :, :] = bias[...]

    @pl.when((step == 0) & (core == 0))
    def _():
        put(0, mine, False)
        put(half, other, True)

    @pl.when((step == 0) & (core == 1))
    def _():
        put(0, other, False)
        put(half, mine, True)

    heads = absorb_key.shape[0]
    latent_size = absorb_key.shape[2]
    queries = []
    for h in range(heads):
        lat = dot(q_nope[:, h * NOPE : (h + 1) * NOPE], absorb_key[h]).astype(BF16)
        rope = q_rope[:, h * ROPE : (h + 1) * ROPE]
        queries.append(jnp.concatenate([lat, rope, jnp.ones((rows, 16), BF16)], axis=1))
    queries = jnp.concatenate(queries, axis=0)
    scores = dot(queries, keys[...])
    shape = (heads * rows, block)
    query = lax.rem(lax.broadcasted_iota(jnp.int32, shape, 0), rows)
    allowed = lax.broadcasted_iota(jnp.int32, shape, 1) <= query
    own = jnp.where(allowed, scores[:, :block], LOW_SCORE)
    scores = jnp.concatenate([own, scores[:, block:]], axis=1)
    top = jnp.max(scores, axis=1, keepdims=True)
    factor = LOG2E * (NOPE + ROPE) ** (-0.5)
    weights = jnp.exp2((scores - top) * factor)
    norm = jnp.sum(weights, axis=1, keepdims=True)
    lat_out = dot(weights.astype(BF16), keys[:latent_size, :], 1, 1)
    lat_out = (lat_out / norm).astype(BF16)
    outs = [
        dot(lat_out[h * rows : (h + 1) * rows], absorb_value[h]).astype(BF16)
        for h in range(heads)
    ]
    for k, load in enumerate(loads):

        @pl.when(step == k)
        def _():
            load.wait()

    part = dot(jnp.concatenate(outs, axis=1), weight[step])

    @pl.when(step == 0)
    def _():
        total[...] = part

    @pl.when(step > 0)
    def _():
        total[...] += part

    @pl.when(step == pl.num_programs(0) - 1)
    def _():
        width = own_out.shape[2]
        for d in range(NY):
            chunk = lax.rem(row_y + d, NY) * 2
            own = pl.multiple_of((chunk + core) * width, 128)
            far = pl.multiple_of((chunk + 1 - core) * width, 128)
            own_out[d] = total[:, pl.ds(own, width)]
            core_out[d] = total[:, pl.ds(far, width)].astype(BF16)


def attention(place, bias, mine, other, q_nope, q_rope, absorb_key, absorb_value, out_proj):
    rows = q_nope.shape[0]
    head_count = absorb_key.shape[0]
    latent_size = absorb_key.shape[2]
    width = out_proj.shape[1]
    per = 4
    key_count = bias.shape[1]
    depth = 2 * mine.shape[0] + bias.shape[0]
    fixed = lambda shape: pl.BlockSpec(shape, lambda i: (0,) * len(shape))
    chunk = (NY, rows, width // (2 * NY))
    return pl.pallas_call(
        attention_kernel,
        grid=(head_count // per,),
        in_specs=[
            pl.BlockSpec(memory_space=pltpu.SMEM),
            fixed(bias.shape),
            fixed(mine.shape),
            fixed(other.shape),
            pl.BlockSpec((rows, per * NOPE), lambda i: (0, i)),
            pl.BlockSpec((rows, per * ROPE), lambda i: (0, i)),
            pl.BlockSpec((per,) + absorb_key.shape[1:], lambda i: (i, 0, 0)),
            pl.BlockSpec((per,) + absorb_value.shape[1:], lambda i: (i, 0, 0)),
            pl.BlockSpec(memory_space=pltpu.HBM),
        ],
        out_specs=[fixed(chunk), fixed(chunk)],
        out_shape=[
            jax.ShapeDtypeStruct(chunk, F32),
            jax.ShapeDtypeStruct(chunk, BF16),
        ],
        scratch_shapes=[
            pltpu.VMEM((depth, key_count), BF16),
            pltpu.VMEM((rows, width), F32),
            pltpu.VMEM((head_count // per, per * VDIM, width), BF16),
            pltpu.SemaphoreType.DMA((head_count // per,)),
        ],
        compiler_params=pltpu.CompilerParams(vmem_limit_bytes=60 * 1024 * 1024),
        cost_estimate=pl.CostEstimate(
            flops=2 * rows * head_count * key_count * (depth + latent_size)
            + 2 * rows * head_count * VDIM * width,
            bytes_accessed=out_proj.size * 2 + 4 * mine.size,
            transcendentals=rows * head_count * key_count,
        ),
        name="attention",
    )(place, bias, mine, other, q_nope, q_rope, absorb_key, absorb_value, out_proj)


FIRST_CUTS = ((1, 0, 1792), (3, 0, 1792))
LATER_CUTS = ((2, 0, 1152), (2, 1152, 1792))


def cut_kernel(cuts, place, gate, up, down, *rest):
    outs, sems = rest[:-1], rest[-1]
    part = gate.shape[1]
    depth = gate.shape[0] // NY
    copies = []
    for out, (d, first, _) in zip(outs, cuts):
        start = pl.multiple_of(lax.rem(place[2] + d, NY) * depth + first, 64)
        for k, source in enumerate((gate, up)):
            copies.append(
                (source.at[pl.ds(start, out.shape[0]), :], out.at[:, k * part : (k + 1) * part])
            )
    for d, out in enumerate(outs[len(cuts) :]):
        start = pl.multiple_of(lax.rem(place[2] + d + 1, NY) * depth, 128)
        copies.append((down.at[:, pl.ds(start, depth)], out))
    copies = [pltpu.make_async_copy(a, b, sems.at[i]) for i, (a, b) in enumerate(copies)]
    for copy in copies:
        copy.start()
    for copy in copies:
        copy.wait()


def cut_weights(name, cuts, down_count, place, gate, up, down):
    hbm = pl.BlockSpec(memory_space=pltpu.HBM)
    outs = pl.pallas_call(
        functools.partial(cut_kernel, cuts),
        in_specs=[pl.BlockSpec(memory_space=pltpu.SMEM), hbm, hbm, hbm],
        out_shape=[
            jax.ShapeDtypeStruct((end - first, 2 * gate.shape[1]), BF16) for _, first, end in cuts
        ]
        + [jax.ShapeDtypeStruct((down.shape[0], down.shape[1] // NY), BF16)] * down_count,
        scratch_shapes=[pltpu.SemaphoreType.DMA((2 * len(cuts) + down_count,))],
        compiler_params=pltpu.CompilerParams(vmem_limit_bytes=60 * 1024 * 1024),
        cost_estimate=pl.CostEstimate(
            flops=0, bytes_accessed=4 * gate.size, transcendentals=0
        ),
        name=name,
    )(place, gate, up, down)
    return outs[: len(cuts)], outs[len(cuts) :]


def first_cut_kernel(place, latent, rope, routes, gate, up, *rest):
    outs, piece, sems = rest[:-2], rest[-2], rest[-1]
    part = gate.shape[1]
    depth = gate.shape[0] // NY
    copies = []
    for out, (d, _, _) in zip(outs, FIRST_CUTS):
        start = pl.multiple_of(lax.rem(place[2] + d, NY) * depth, 128)
        for k, source in enumerate((gate, up)):
            copies.append(
                pltpu.make_async_copy(
                    source.at[pl.ds(start, depth), :],
                    out.at[:, k * part : (k + 1) * part],
                    sems.at[len(copies)],
                )
            )
    for copy in copies:
        copy.start()
    size, rows = latent.shape
    half = (size + rope.shape[0]) // 2

    @pl.when(place[0] == 0)
    def _():
        piece[:half, :] = latent[:half, :]

    @pl.when(place[0] != 0)
    def _():
        piece[: size - half, :] = latent[half:, :]
        piece[size - half : half, :] = rope[...]

    expert = lax.broadcasted_iota(jnp.int32, (piece.shape[0] - half, rows), 0)
    named = jnp.zeros(expert.shape, F32)
    for k in range(routes.shape[0]):
        picked = jnp.broadcast_to(routes[k : k + 1, :], expert.shape) == expert
        named = jnp.where(picked, 1.0, named)
    piece[half:, :] = named.astype(BF16)
    for copy in copies:
        copy.wait()


def first_cut(place, latent, rope, routes, gate, up, experts):
    hbm = pl.BlockSpec(memory_space=pltpu.HBM)
    vmem = pl.BlockSpec(memory_space=pltpu.VMEM)
    half = (latent.shape[0] + rope.shape[0]) // 2
    shape = (gate.shape[0] // NY, 2 * gate.shape[1])
    *cuts, piece = pl.pallas_call(
        first_cut_kernel,
        in_specs=[pl.BlockSpec(memory_space=pltpu.SMEM), vmem, vmem, vmem, hbm, hbm],
        out_shape=[jax.ShapeDtypeStruct(shape, BF16)] * len(FIRST_CUTS)
        + [jax.ShapeDtypeStruct((half + experts, latent.shape[1]), BF16)],
        scratch_shapes=[pltpu.SemaphoreType.DMA((2 * len(FIRST_CUTS),))],
        compiler_params=pltpu.CompilerParams(vmem_limit_bytes=60 * 1024 * 1024),
        cost_estimate=pl.CostEstimate(
            flops=0, bytes_accessed=4 * gate.size, transcendentals=0
        ),
        name="first_cut",
    )(place, latent, rope, routes, gate, up)
    return cuts, piece


def unpack_kernel(place, first, second, third, down, own, far, kept, sem):
    rows, depth = kept.shape
    width = depth // 2
    start = pl.multiple_of(place[2] * depth, 128)
    copy = pltpu.make_async_copy(down.at[:, pl.ds(start, depth)], kept, sem)
    copy.start()
    near = pl.multiple_of(place[0] * width, 128)
    away = pl.multiple_of((1 - place[0]) * width, 128)
    for d, ref in ((1, first), (2, second), (3, third), (0, kept)):
        if d == 0:
            copy.wait()
        own[d * rows : (d + 1) * rows, :] = ref[:, pl.ds(near, width)]
        far[d * rows : (d + 1) * rows, :] = ref[:, pl.ds(away, width)]


def unpack(place, moved, down):
    rows, depth = moved[0].shape
    vmem = pl.BlockSpec(memory_space=pltpu.VMEM)
    return pl.pallas_call(
        unpack_kernel,
        in_specs=[pl.BlockSpec(memory_space=pltpu.SMEM), vmem, vmem, vmem]
        + [pl.BlockSpec(memory_space=pltpu.HBM)],
        out_shape=[jax.ShapeDtypeStruct((NY * rows, depth // 2), BF16)] * 2,
        scratch_shapes=[pltpu.VMEM((rows, depth), BF16), pltpu.SemaphoreType.DMA],
        compiler_params=pltpu.CompilerParams(vmem_limit_bytes=12 * 1024 * 1024),
        cost_estimate=pl.CostEstimate(
            flops=0, bytes_accessed=16 * rows * depth, transcendentals=0
        ),
        name="unpack",
    )(place, *moved, down)


def slots_of(line, capacity):
    ids = lax.broadcasted_iota(jnp.int32, (capacity, line.shape[1]), 0)
    return jnp.broadcast_to(line, ids.shape) == ids


def fill_kernel(slot, t0, t1, t2, t3, *outs):
    for e, out in enumerate(outs):
        capacity = out.shape[0] // NY
        for d, ref in enumerate((t0, t1, t2, t3)):
            at = d * 4 + e
            placed = slots_of(slot[at : at + 1, :], capacity).astype(BF16)
            out[d * capacity : (d + 1) * capacity, :] = dot(placed, ref[...]).astype(BF16)


def fill(slot, tokens, capacity):
    rows, width = tokens[0].shape
    return pl.pallas_call(
        fill_kernel,
        out_shape=[jax.ShapeDtypeStruct((4 * capacity, width), BF16)] * 4,
        compiler_params=pltpu.CompilerParams(vmem_limit_bytes=16 * 1024 * 1024),
        cost_estimate=pl.CostEstimate(
            flops=32 * capacity * rows * width,
            bytes_accessed=8 * rows * width + 32 * capacity * width,
            transcendentals=0,
        ),
        name="fill",
    )(slot, *tokens)


def mix_kernel(slot, gates, r0, r1, r2, r3, own, *far):
    capacity = r0.shape[0] // 4
    for d in range(4):
        high, low, rows = [], [], []
        for e, ref in enumerate((r0, r1, r2, r3)):
            at = d * 4 + e
            placed = slots_of(slot[at : at + 1, :], capacity)
            value = jnp.where(placed, jnp.broadcast_to(gates[at : at + 1, :], placed.shape), 0.0)
            first = value.astype(BF16)
            high.append(first)
            low.append((value - first.astype(F32)).astype(BF16))
            rows.append(ref[d * capacity : (d + 1) * capacity, :])
        rows = jnp.concatenate(rows, axis=0)
        total = dot(jnp.concatenate(high, axis=0), rows, 0, 0)
        total = total + dot(jnp.concatenate(low, axis=0), rows, 0, 0)
        if d == 0:
            own[...] = total
        else:
            far[d - 1][...] = total.astype(BF16)


def mix(slot, gates, returned):
    width = returned[0].shape[1]
    rows = slot.shape[1]
    return pl.pallas_call(
        mix_kernel,
        out_shape=[jax.ShapeDtypeStruct((rows, width), F32)]
        + [jax.ShapeDtypeStruct((rows, width), BF16)] * 3,
        compiler_params=pltpu.CompilerParams(vmem_limit_bytes=16 * 1024 * 1024),
        cost_estimate=pl.CostEstimate(
            flops=16 * returned[0].size * rows,
            bytes_accessed=8 * returned[0].size + 10 * rows * width,
            transcendentals=0,
        ),
        name="mix",
    )(slot, gates, *returned)


def gather_rows(place, held, mine, other):
    depth = mine[0].shape[1]
    block = mine[0].shape[0] // 4
    near = pl.multiple_of(place[0] * depth, 128)
    away = pl.multiple_of((1 - place[0]) * depth, 128)
    for e in range(4):
        for d in range(4):
            at = (e * 4 + d) * block
            held[at : at + block, pl.ds(near, depth)] = mine[e][d * block : (d + 1) * block, :]
            held[at : at + block, pl.ds(away, depth)] = other[d][e * block : (e + 1) * block, :]


def dot_parts(held, parts):
    total, start = 0.0, 0
    for part in parts:
        total = total + dot(held[:, start : start + part.shape[0]], part[...])
        start += part.shape[0]
    return total


def gate_up_kernel(place, *refs):
    mine, other, parts, inv_gain, near_stats, far_stats = (
        refs[:4], refs[4:8], refs[8:12], refs[12], refs[13], refs[14]
    )
    far_outs, own_square, stats, held = refs[15:18], refs[18], refs[19], refs[20]
    rows, depth = held.shape
    wide = own_square.shape[1]
    gather_rows(place, held, mine, other)
    row = lax.broadcasted_iota(jnp.int32, (8, wide), 0)
    picked = jnp.zeros((8, wide), F32)
    for q in range(rows // wide):
        lines = []
        for k in range(wide // 128):
            at = q * wide + k * 128
            sums = jnp.zeros((128, 128), F32)
            for c in range(0, depth, 128):
                value = held[at : at + 128, c : c + 128].astype(F32) * inv_gain[:, c : c + 128]
                sums = sums + value * value
            lines.append(jnp.sum(jnp.transpose(sums), axis=0, keepdims=True))
        line = jnp.broadcast_to(jnp.concatenate(lines, axis=1), (8, wide))
        picked = jnp.where(lax.rem(row, 4) == q, line, picked)
    own_square[...] = picked
    high = picked.astype(BF16)
    low = (picked - high.astype(F32)).astype(BF16)
    both = jnp.where(row < 4, high.astype(F32), low.astype(F32))
    sums = near_stats[...] + far_stats[...]
    stats[...] = sums
    high = sums.astype(BF16).astype(F32)
    pair = jnp.concatenate([high, sums - high], axis=1)
    both = jnp.concatenate([both, pair], axis=0).astype(BF16)
    for d in range(1, NY):
        out = far_outs[d - 1]
        chosen = (parts[:1], parts[1:3], parts[3:])[d - 1]
        out[:rows, :] = dot_parts(held, chosen).astype(BF16)
        out[rows:, :] = both


def gate_up(place, mine, other, parts, inv_gain, near_stats, far_stats):
    rows, depth = 4 * mine[0].shape[0], 2 * mine[0].shape[1]
    wide = parts[0].shape[1]
    vmem = pl.BlockSpec(memory_space=pltpu.VMEM)
    return pl.pallas_call(
        gate_up_kernel,
        in_specs=[pl.BlockSpec(memory_space=pltpu.SMEM)] + [vmem] * 15,
        out_shape=[jax.ShapeDtypeStruct((rows + 32, wide), BF16)] * 3
        + [
            jax.ShapeDtypeStruct((8, wide), F32),
            jax.ShapeDtypeStruct(near_stats.shape, F32),
        ],
        scratch_shapes=[pltpu.VMEM((rows, depth), BF16)],
        compiler_params=pltpu.CompilerParams(vmem_limit_bytes=60 * 1024 * 1024),
        cost_estimate=pl.CostEstimate(
            flops=8 * rows * depth * wide, bytes_accessed=4 * rows * depth, transcendentals=0
        ),
        name="gate_up",
    )(place, *mine, *other, *parts, inv_gain, near_stats, far_stats)


def gate_up_own_kernel(place, *refs):
    mine, other, (gate, up, out, held, weight, sems) = refs[:4], refs[4:8], refs[8:]
    depth = weight.shape[0]
    part = gate.shape[1]
    start = pl.multiple_of(place[2] * depth, 128)
    copies = [
        pltpu.make_async_copy(
            source.at[pl.ds(start, depth), :],
            weight.at[:, k * part : (k + 1) * part],
            sems.at[k],
        )
        for k, source in enumerate((gate, up))
    ]
    for copy in copies:
        copy.start()
    gather_rows(place, held, mine, other)
    for copy in copies:
        copy.wait()
    out[...] = dot(held[...], weight[...])


def gate_up_own(place, mine, other, gate, up):
    rows, depth = 4 * mine[0].shape[0], 2 * mine[0].shape[1]
    wide = 2 * gate.shape[1]
    vmem = pl.BlockSpec(memory_space=pltpu.VMEM)
    hbm = pl.BlockSpec(memory_space=pltpu.HBM)
    return pl.pallas_call(
        gate_up_own_kernel,
        in_specs=[pl.BlockSpec(memory_space=pltpu.SMEM)] + [vmem] * 8 + [hbm] * 2,
        out_shape=jax.ShapeDtypeStruct((rows, wide), F32),
        scratch_shapes=[
            pltpu.VMEM((rows, depth), BF16),
            pltpu.VMEM((depth, wide), BF16),
            pltpu.SemaphoreType.DMA((2,)),
        ],
        compiler_params=pltpu.CompilerParams(vmem_limit_bytes=24 * 1024 * 1024),
        cost_estimate=pl.CostEstimate(
            flops=40 * rows * depth * wide, bytes_accessed=4 * rows * depth, transcendentals=0
        ),
        name="own_part",
    )(place, *mine, *other, gate, up)


def down_kernel(mine, other, own_down, far_down, o0, o1, o2, o3, turned):
    block = o0.shape[0] // 4
    for e in range(4):
        for d in range(4):
            turned[(e * 4 + d) * block : (e * 4 + d + 1) * block, :] = other[
                (d * 4 + e) * block : (d * 4 + e + 1) * block, :
            ]
    for e, out in enumerate((o0, o1, o2, o3)):
        at = slice(e * 4 * block, (e + 1) * 4 * block)
        value = dot(mine[at, :], own_down[...]) + dot(turned[at, :], far_down[...])
        out[...] = value.astype(BF16)


def down(mine, other, own_down, far_down):
    rows, depth = mine.shape
    width = own_down.shape[1]
    return pl.pallas_call(
        down_kernel,
        out_shape=[jax.ShapeDtypeStruct((rows // 4, width), BF16)] * 4,
        scratch_shapes=[pltpu.VMEM((rows, depth), BF16)],
        compiler_params=pltpu.CompilerParams(vmem_limit_bytes=16 * 1024 * 1024),
        cost_estimate=pl.CostEstimate(
            flops=4 * rows * depth * width,
            bytes_accessed=4 * rows * depth + 6 * rows * width,
            transcendentals=0,
        ),
        name="down",
    )(mine, other, own_down, far_down)


def hidden_kernel(full, own, own_square, stats, first, second, third, out, summed):
    rows, wide = own.shape
    far = (first, second, third)
    square = own_square[0:8, :]
    low = jnp.zeros((8, wide), F32)
    total = stats[...]
    for ref in far:
        both = ref[rows : rows + 32, :].astype(F32)
        low = low + both[0:8]
        total = total + both[8:32, :128] + both[8:32, 128:]
    summed[...] = total
    row = lax.broadcasted_iota(jnp.int32, (8, wide), 0)
    square = jnp.where(row < 4, square, 0.0) + low
    square = square[0:4] + square[4:8]
    scale = lax.rsqrt(square / full + EPS)
    part = wide // 2
    for k in range(rows // part):
        line = scale[k // 2 : k // 2 + 1, k % 2 * part : (k % 2 + 1) * part]
        factor = jnp.transpose(jnp.broadcast_to(line, (part, part)))
        at = slice(k * part, (k + 1) * part)
        value = own[at, :]
        for ref in far:
            value = value + ref[at, :].astype(F32)
        gate = value[:, :part] * factor
        up = value[:, part:] * factor
        out[at, :] = (gate / (1.0 + jnp.exp(-gate)) * up).astype(BF16)


def hidden_of(own, own_square, stats, far, full):
    rows, wide = own.shape
    return pl.pallas_call(
        functools.partial(hidden_kernel, full),
        out_shape=[
            jax.ShapeDtypeStruct((rows, wide // 2), BF16),
            jax.ShapeDtypeStruct(stats.shape, F32),
        ],
        compiler_params=pltpu.CompilerParams(vmem_limit_bytes=12 * 1024 * 1024),
        cost_estimate=pl.CostEstimate(
            flops=8 * rows * wide, bytes_accessed=own.size * 10, transcendentals=rows * wide
        ),
        name="hidden",
    )(own, own_square, stats, *far)


def body(
    x_resid,
    query_nope,
    query_rope,
    latent_kv,
    key_rope,
    absorb_key,
    absorb_value,
    out_proj,
    norm_gain,
    router,
    routes,
    gate_proj,
    up_proj,
    down_proj,
):
    rows, width = x_resid.shape
    experts = lax.axis_size("ctx")
    capacity = 2 * rows * TOP // experts
    full = out_proj.shape[1]
    ctx = lax.axis_index("ctx")
    tp = lax.axis_index("tp")
    core = tp % 2
    row_y = tp // 2
    z, x = ctx // NX, ctx % NX

    place = jnp.stack([core, ctx, row_y]).astype(jnp.int32)

    with jax.named_scope("key_gather"):
        expert_ids = jnp.arange(experts, dtype=jnp.int32)
        half = (latent_kv.shape[0] + key_rope.shape[0]) // 2
    with jax.named_scope("weights_gate_up"):
        weights = (gate_proj[0], up_proj[0], down_proj[0])
        cuts, piece = first_cut(
            place, latent_kv, key_rope, routes.T, gate_proj[0], up_proj[0], experts
        )
        first = shift(cuts[0], dy=1)
        third = shift(cuts[1], dy=3)

    with jax.named_scope("key_gather"):
        pieces = [piece] + [shift(piece, (d, 0), (0, d)) for d in range(1, 4)]
        line = jnp.concatenate([p[:half] for p in pieces], axis=1)
        masks = jnp.stack([p[half:] for p in pieces])
        named = masks[0] > 0

    with jax.named_scope("weights_gate_up"):
        line, weights = lax.optimization_barrier((line, weights))
        cuts, down_cuts = cut_weights("cut_later", LATER_CUTS, 3, place, *weights)

    with jax.named_scope("key_gather"):
        mine = jnp.concatenate(
            [line] + [shift(line, (0, d), (d, 0)) for d in range(1, 4)], axis=1
        )
        inv_gain = lax.dynamic_slice_in_dim(norm_gain, row_y * 2 * width, 2 * width, 0)
        inv_gain = (1.0 / inv_gain.astype(F32)).reshape(1, 2 * width)
        mine, first, third, cuts, down_cuts, inv_gain = lax.optimization_barrier(
            (mine, first, third, cuts, down_cuts, inv_gain)
        )
        other = shift(mine, dc=1)
        order = jnp.arange(16, dtype=jnp.int32)
        source = (z - order % 4 + 4) % 4 * 4 + (x - order // 4 + 4) % 4
        bias = jnp.where(source <= ctx, 0.0, LOW_SCORE)[None, :, None]
        bias = jnp.where(order[:, None, None] == 0, bias, 0.0)
        bias = jnp.broadcast_to(bias, (16, 16, rows)).reshape(16, 16 * rows).astype(BF16)

    with jax.named_scope("slots"):
        token = jnp.arange(rows, dtype=jnp.int32)
        earlier = (token[:, None] < token[None, :]).astype(BF16)
        slot = jnp.dot(
            masks.reshape(4 * experts, rows), earlier, preferred_element_type=F32
        ).reshape(4, experts, rows)
        slot = jnp.where(masks > 0, slot, -1.0)
        step = jnp.arange(4, dtype=jnp.int32)
        passing = jnp.where(core == 0, z * NX + (x + step) % NX, (z + step) % NZ * NX + x)
        passing = passing[None, :, None, None] == expert_ids[None, None, :, None]

        def pick(values):
            values = jnp.where(passing, values[:, None], 0.0)
            return jnp.sum(values, axis=2).reshape(16, rows)

        slot = pick(slot).astype(jnp.int32)

    with jax.named_scope("weights_gate_up"):
        second0 = shift(cuts[0], dy=2)

    own_part, core_part = attention(
        place, bias, mine, other, query_nope, query_rope, absorb_key, absorb_value, out_proj
    )

    own_part, core_part, second0 = lax.optimization_barrier((own_part, core_part, second0))

    with jax.named_scope("attn_sum"):
        pair = own_part + shift(core_part, dc=1).astype(F32)
        pair_low = pair.astype(BF16)
        resid = x_resid.astype(F32) + pair[0]
        for d in range(1, NY):
            resid = resid + shift(pair_low[d], dy=d).astype(F32)

    with jax.named_scope("dispatch"):
        col_start = tp * width
        gain = lax.dynamic_slice_in_dim(norm_gain, col_start, width, 0).astype(F32)
        scaled = resid * gain[None, :]
        outgoing = scaled.astype(BF16)
        router_cols = lax.dynamic_slice_in_dim(router, col_start, width, 1).astype(F32)
        outgoing, late_down, late = lax.optimization_barrier((outgoing, down_cuts, cuts[1]))
        tokens = [outgoing] + [shift(outgoing, (d, 0), (0, d)) for d in range(1, 4)]

    with jax.named_scope("weights_down"):
        moved = [shift(late_down[0], dy=1), None, shift(late_down[2], dy=3)]
        tokens, moved, late, far_cut = lax.optimization_barrier(
            (tokens, moved, late, late_down[1])
        )
        moved[1] = shift(far_cut, dy=2)
        second1 = shift(late, dy=2)

    with jax.named_scope("gates"):
        scaled, resid_late = lax.optimization_barrier((scaled, resid))
        logits = lax.dot_general(
            router_cols, scaled, (((1,), (1,)), ((), ())), precision=lax.Precision.HIGHEST
        )
        squares = jnp.sum(resid_late * resid_late, axis=1)[None, :]
        stats = jnp.concatenate([logits, jnp.broadcast_to(squares, (8, rows))], axis=0)
        far_stats = shift(stats, dc=1)

    with jax.named_scope("dispatch"):
        filled = fill(slot, tokens, capacity)
        arrived = [filled[0]] + [shift(filled[e], (0, e), (e, 0)) for e in range(1, 4)]
        arrived, moved[1], second1, far_stats = lax.optimization_barrier(
            (arrived, moved[1], second1, far_stats)
        )
        far_cols = [shift(block, dc=1) for block in arrived]

    with jax.named_scope("experts"):
        parts = (first, second0, second1, third)
        *far, own_square, stats = gate_up(
            place, arrived, far_cols, parts, inv_gain, stats, far_stats
        )
        moved, arrived, own_square = lax.optimization_barrier((moved, arrived, own_square))
        far = [shift(far[d - 1], dy=-d) for d in range(1, NY)]
        own = gate_up_own(place, arrived, far_cols, gate_proj[0], up_proj[0])

    with jax.named_scope("weights_down"):
        own_down, far_down = unpack(place, moved, down_proj[0])
        far_down = shift(far_down, dc=1)
        own, own_down, far_down = lax.optimization_barrier((own, own_down, far_down))

    with jax.named_scope("experts"):
        hidden, summed = hidden_of(own, own_square, stats, far, float(full))
        hidden = jnp.concatenate(
            [hidden] + [shift(hidden, dy=d) for d in range(1, NY)], axis=1
        )

    with jax.named_scope("gates"):
        inv_rms = lax.rsqrt(summed[experts] / full + EPS)
        gates = jnp.where(named, jax.nn.sigmoid(summed[:experts] * inv_rms[None, :]), 0.0)
        gates = ROUTE_SCALE * gates / jnp.sum(gates, axis=0, keepdims=True)
        gates = [gates] + [shift(gates, (d, 0), (0, d)) for d in range(1, 4)]
        hidden, gates = lax.optimization_barrier((hidden, gates))
        gates = pick(jnp.stack(gates))

    with jax.named_scope("experts"):
        far_hidden = shift(hidden, dc=1)
        result = down(hidden, far_hidden, own_down, far_down)

    with jax.named_scope("combine"):
        result = [result[0]] + [shift(result[e], (0, -e), (-e, 0)) for e in range(1, 4)]
        own_sum, *far_sum = mix(slot, gates, result)
        total = resid + own_sum
        for d in range(1, 4):
            total = total + shift(far_sum[d - 1], (-d, 0), (0, -d)).astype(F32)
        return total.astype(BF16)


def solution(mesh):
    return jax.shard_map(
        body,
        mesh=mesh,
        in_specs=(
            P("ctx", "tp"),
            P("ctx", "tp"),
            P("ctx", "tp"),
            P(None, "ctx"),
            P(None, "ctx"),
            P("tp", None, None),
            P("tp", None, None),
            P("tp", None),
            P(),
            P(),
            P("ctx", None),
            P("ctx", None, "tp"),
            P("ctx", None, "tp"),
            P("ctx", "tp", None),
        ),
        out_specs=P("ctx", "tp"),
        check_vma=False,
    )
```
